512 devices in a mesh: member: 16 (over z, x_hi), lat: 4 (over x_lo, core), lon: 8 (over y).
Axes of the slice: x: 4 (x_hi: 2, x_lo: 2; x = x_hi * 2 + x_lo), y: 8, z: 8, core: 2. Of those that a mesh axis runs over, the one named last changes fastest.
Arguments:
- inputs: bfloat16 [16, 16, 64, 1024], P('member', None, 'lat', 'lon'), may hold values from -6 to 6
- target: bfloat16 [16, 64, 1024], P(None, 'lat', 'lon'), may hold values from -6 to 6
- conv_in: bfloat16 [9, 128, 16], replicated, may hold values from -0.5 to 0.5
- bias_in: float32 [128], replicated, may hold values from -3 to 3
- conv_out: bfloat16 [9, 16, 128], replicated, may hold values from -0.1875 to 0.1875
Outputs:
- input_grad: float32 [16, 16, 64, 1024], P('member', None, 'lat', 'lon')
- conv_in_grad: float32 [9, 128, 16], replicated
- conv_out_grad: float32 [9, 16, 128], replicated
The draws below stay inside these ranges and needn't reach their ends.
All inputs are finite; a program needn't handle non-finite values.
Results may differ from the reference program's by a relative error of at most 0.013.
Values may be sent and summed in bfloat16 or wider, within the bound.
A program may use at most 64 MiB of HBM per device.

```python
import math
import jax
import jax.numpy as jnp
from jax import lax

LEV = 16
C = 128
MEMBERS = 16
NLAT = 64
NLON = 1024


def block_levels(own_key, dims, cuts, least, largest):
    def one(dim, parts):
        heights = jax.random.uniform(jax.random.fold_in(jax.random.fold_in(own_key, 6), dim), (parts,), jnp.float32, least / len(cuts), largest / len(cuts))
        return jnp.repeat(jnp.exp(heights), dims[dim] // parts).reshape((-1,) + (1,) * (len(dims) - dim - 1))

    factor_of = one(*cuts[0])
    for cut in cuts[1:]:
        factor_of = factor_of * one(*cut)
    return factor_of


def normal_values(rng, shape, scale, reach, pieces=(), kind=jnp.bfloat16):
    factor_of = block_levels(rng, shape, pieces, -0.22, 0.18) if pieces else 1.0
    values = jax.random.normal(rng, shape, jnp.float32) * scale * factor_of
    return jnp.minimum(jnp.maximum(values, -reach), reach).astype(kind)


def setup_inputs(seed: int = 0) -> dict:
    streams_of = jax.random.split(jax.random.key(seed), 6)
    return {
        "inputs": normal_values(streams_of[0], (MEMBERS, LEV, NLAT, NLON), 1.0, 6.0, ((0, 16), (2, 4), (3, 8))),
        "target": normal_values(streams_of[1], (LEV, NLAT, NLON), 1.0, 6.0, ((1, 4), (2, 8))),
        "conv_in": normal_values(streams_of[2], (9, C, LEV), (9 * LEV) ** -0.5, 0.5),
        "bias_in": normal_values(streams_of[3], (C,), 0.5, 3.0, (), jnp.float32),
        "conv_out": normal_values(streams_of[4], (9, LEV, C), (9 * C) ** -0.5, 0.1875),
    }


def kernel_slope(difference):
    return difference / jnp.sqrt(difference * difference + 0.25)

def silu_slope(hidden_pre):
    sigmoid = jax.nn.sigmoid(hidden_pre)
    return sigmoid * (1.0 + hidden_pre * (1.0 - sigmoid))

def pad_cycle(field):
    field = jnp.concatenate([field[:, :, -1:], field, field[:, :, :1]], axis=2)
    return jnp.pad(field, ((0, 0), (1, 1), (0, 0)))

def stencil(weight, padded, flip, row_count, col_count):
    running = None
    for row_step in (-1, 0, 1):
        for col_step in (-1, 0, 1):
            offset = 3 * (row_step + 1) + (col_step + 1)
            matrix = weight[offset] if flip == 1 else weight[offset].T
            start_row = 1 + flip * row_step
            start_col = 1 + flip * col_step
            window = padded[:, start_row:start_row + row_count, start_col:start_col + col_count]
            window = window.reshape(padded.shape[0], row_count * col_count)
            term = jnp.dot(matrix, window, preferred_element_type=jnp.float32)
            running = term if running is None else running + term
    return running.reshape(-1, row_count, col_count)

def reference(inputs, target, conv_in, bias_in, conv_out):
    scale = 1.0 / math.sqrt(MEMBERS * NLAT * NLON)
    coupling = (1.0 - 0.05 / MEMBERS) / (MEMBERS - 1)
    target_wide = target.astype(jnp.float32)

    def forward(member_field):
        hidden_pre = stencil(conv_in, pad_cycle(member_field), 1, NLAT, NLON) + bias_in[:, None, None]
        activated = jax.nn.silu(hidden_pre).astype(jnp.bfloat16)
        summed = member_field.astype(jnp.float32) + stencil(conv_out, pad_cycle(activated), 1, NLAT, NLON)
        return summed.astype(jnp.bfloat16)
    predictions = lax.map(forward, inputs)

    def backward(member_pair):
        member_field, prediction = member_pair
        own_pred = prediction.astype(jnp.float32)

        def accumulate(running, other_pred):
            return (running + kernel_slope(own_pred - other_pred.astype(jnp.float32)), None)
        spread, unused_out = lax.scan(accumulate, jnp.zeros(own_pred.shape, jnp.float32), predictions)
        grad_pred = (kernel_slope(own_pred - target_wide) - coupling * spread).astype(jnp.bfloat16)
        padded_in = pad_cycle(member_field)
        hidden_pre = stencil(conv_in, padded_in, 1, NLAT, NLON) + bias_in[:, None, None]
        activated = jax.nn.silu(hidden_pre).astype(jnp.bfloat16)
        padded_act = pad_cycle(activated)
        grad_act = stencil(conv_out, pad_cycle(grad_pred), -1, NLAT, NLON)
        grad_hidden = (grad_act * silu_slope(hidden_pre)).astype(jnp.bfloat16)
        grad_field = grad_pred.astype(jnp.float32) + stencil(conv_in, pad_cycle(grad_hidden), -1, NLAT, NLON)
        flat_hidden = grad_hidden.reshape(grad_hidden.shape[0], -1)
        flat_pred = grad_pred.reshape(grad_pred.shape[0], -1)
        in_terms = []
        out_terms = []
        for row_step in (-1, 0, 1):
            for col_step in (-1, 0, 1):
                in_window = padded_in[:, 1 + row_step:1 + row_step + NLAT, 1 + col_step:1 + col_step + NLON]
                act_window = padded_act[:, 1 + row_step:1 + row_step + NLAT, 1 + col_step:1 + col_step + NLON]
                in_window = in_window.reshape(in_window.shape[0], -1)
                act_window = act_window.reshape(act_window.shape[0], -1)
                in_terms.append(jnp.dot(flat_hidden, in_window.T, preferred_element_type=jnp.float32))
                out_terms.append(jnp.dot(flat_pred, act_window.T, preferred_element_type=jnp.float32))
        return (grad_field, jnp.stack(in_terms), jnp.stack(out_terms))
    input_grad, in_parts, out_parts = lax.map(backward, (inputs, predictions))
    return (input_grad, lax.optimization_barrier(jnp.sum(in_parts, axis=0)) * scale, lax.optimization_barrier(jnp.sum(out_parts, axis=0)) * scale)
```

```python
import functools
import math

import jax
import jax.numpy as jnp
from jax import lax
from jax.experimental import pallas as pl
from jax.experimental.pallas import tpu as pltpu
from jax.sharding import PartitionSpec as P

MESH = pl.DeviceIdType.MESH
F32 = jnp.float32
BF16 = jnp.bfloat16

LEV = 16
C = 128
ROWS = 16
COLS = 128
HALO = 4
PITCH = COLS + 2 * HALO
FLAT = 26 * 128
LEAD = 128
OFFSETS = [(di, dj) for di in (-1, 0, 1) for dj in (-1, 0, 1)]
SHIFTS = [di * PITCH + dj for di, dj in OFFSETS]
PRED_FIRST = 2
PRED_TILES = 22
TAPS = 9 * LEV
PART = TAPS // 8


def ring_order(count):
    return sorted(range(count), key=lambda d: (-min(d, count - d), d))


def kernel(
    sizes,
    x_hbm,
    t_hbm,
    w_in_hbm,
    bias_ref,
    w_out_hbm,
    field_hbm,
    gin_ref,
    gout_ref,
    x16,
    t16,
    win16,
    wout16,
    rows32,
    xf,
    w_in,
    w_in_t,
    w_out_t,
    bias,
    side_send,
    band_send,
    side_recv,
    band_recv,
    xc,
    pre,
    act,
    act_own,
    taps,
    pred_send,
    pred_recv,
    target_tiles,
    grad_send,
    grad_recv,
    gp,
    gc,
    gh,
    field,
    part_sum,
    part_recv,
    lon_recv,
    mem_recv,
    all_recv,
    load_sem,
    send_sem,
    recv_sem,
):
    members, lats, lons = sizes
    zs = members // 2
    quads = 2 * lats
    share = -(-PRED_TILES // members)
    chunk = -(-PART // quads)
    me_m = lax.axis_index("member")
    me_a = lax.axis_index("lat")
    me_o = lax.axis_index("lon")
    me_z = me_m // 2
    me_h = me_m % 2
    me_q = me_h * lats + me_a

    loads = [
        pltpu.make_async_copy(src, dst, load_sem.at[i])
        for i, (src, dst) in enumerate(
            ((x_hbm.at[0], x16), (t_hbm, t16), (w_in_hbm, win16), (w_out_hbm, wout16))
        )
    ]
    for load in loads:
        load.start()

    def at(dm_z, dm_h, da, do):
        return (
            ((me_z + dm_z) % zs) * 2 + (me_h + dm_h) % 2,
            (me_a + da + lats) % lats,
            (me_o + do + lons) % lons,
        )

    halo = [(da, do) for da, do in ((-1, -1), (-1, 1), (1, -1), (1, 1), (0, -1), (0, 1), (-1, 0), (1, 0))]
    group_m = [(dz, h) for dz in ring_order(zs) for h in (1, 0) if dz or h]
    group_q = [(h, da) for h in (1, 0) for da in ring_order(lats) if h or da]
    group_o = [d for d in ring_order(lons) if d]
    group_z = [d for d in ring_order(zs) if d]

    barrier = pltpu.get_barrier_semaphore()
    greet = [at(dz, h, 0, 0) for dz, h in group_m]
    greet += [at(0, 0, 0, d) for d in group_o]
    greet += [at(0, h, da, 0) for h, da in group_q]
    greet += [at(0, 0, da, do) for da, do in halo]
    for device in greet:
        pl.semaphore_signal(barrier, inc=1, device_id=device, device_id_type=MESH)

    loads[0].wait()
    loads[1].wait()
    rows32[0:LEV] = x16[...].astype(F32)
    rows32[LEV:] = t16[...].astype(F32)
    for r in range(ROWS):
        start = LEAD + PITCH * (r + HALO) + HALO
        xf[:, start : start + COLS] = rows32[:, r, :]

    def place(first, height, width):
        lane = lax.broadcasted_iota(jnp.int32, (height, width), 1).astype(F32) + float(first)
        row = jnp.floor((lane + 0.5) * (1.0 / PITCH))
        return row, lane - PITCH * row

    left_edge = jnp.zeros((2 * LEV, 128), F32)
    right_edge = jnp.zeros((2 * LEV, 128), F32)
    for t in range(4, 22):
        row, col = place(t * 128, 2 * LEV, 128)
        here = (row >= HALO) & (row < HALO + ROWS)
        tile = xf[:, LEAD + t * 128 : LEAD + t * 128 + 128]
        left_edge += jnp.where(here & (col >= HALO) & (col < 2 * HALO), tile, 0.0)
        right_edge += jnp.where(here & (col >= COLS) & (col < COLS + HALO), tile, 0.0)
    side_send[0] = right_edge.astype(BF16)
    side_send[1] = left_edge.astype(BF16)
    band_send[0] = xf[:, LEAD + 17 * 128 : LEAD + 22 * 128].astype(BF16)
    band_send[1] = xf[:, LEAD + 4 * 128 : LEAD + 9 * 128].astype(BF16)

    loads[2].wait()
    loads[3].wait()
    wide = jnp.concatenate([win16[k].astype(F32) for k in range(9)], axis=1)
    w_in[...] = wide.astype(BF16)
    w_in_t[...] = wide.T.astype(BF16)
    w_out = wout16[...].reshape(TAPS, C)
    w_out_t[...] = w_out.astype(F32).T.astype(BF16)
    bias[...] = jnp.broadcast_to(bias_ref[...], (C, C)).T
    taps[:, 0:128] = jnp.zeros((TAPS, 128), F32)
    taps[:, FLAT - 128 : FLAT] = jnp.zeros((TAPS, 128), F32)
    xf[:, 0:LEAD] = jnp.zeros((2 * LEV, LEAD), F32)
    xf[:, LEAD + FLAT :] = jnp.zeros((2 * LEV, 128), F32)
    gp[...] = jnp.zeros_like(gp)
    target_tiles[...] = jnp.zeros_like(target_tiles)
    pred_send[...] = jnp.zeros_like(pred_send)

    pl.semaphore_wait(barrier, len(greet))

    sends = []

    def send(src, dst, phase, device):
        copy = pltpu.make_async_remote_copy(
            src_ref=src,
            dst_ref=dst,
            send_sem=send_sem.at[phase],
            recv_sem=recv_sem.at[phase],
            device_id=device,
            device_id_type=MESH,
        )
        copy.start()

    def wait_recv(ref, phase):
        pltpu.make_async_remote_copy(
            src_ref=ref,
            dst_ref=ref,
            send_sem=send_sem.at[phase],
            recv_sem=recv_sem.at[phase],
            device_id=(me_m, me_a, (me_o + 1) % lons),
            device_id_type=MESH,
        ).wait_recv()

    def wait_send(ref, phase):
        pltpu.make_async_remote_copy(
            src_ref=ref,
            dst_ref=ref,
            send_sem=send_sem.at[phase],
            recv_sem=recv_sem.at[phase],
            device_id=(me_m, me_a, (me_o + 1) % lons),
            device_id_type=MESH,
        ).wait_send()

    for da in (-1, 1, 0):
        send(side_send.at[0], side_recv.at[0, 1 - da], 0, at(0, 0, da, 1))
        send(side_send.at[1], side_recv.at[1, 1 - da], 0, at(0, 0, da, -1))
    send(band_send.at[0], band_recv.at[0], 1, at(0, 0, 1, 0))
    send(band_send.at[1], band_recv.at[1], 1, at(0, 0, -1, 0))

    wait_recv(side_recv, 0)
    wait_recv(band_recv, 1)

    row_low = jnp.where(me_a == 0, HALO, 0).astype(F32)
    row_high = jnp.where(me_a == lats - 1, HALO + ROWS, ROWS + 2 * HALO).astype(F32)
    sides = [[side_recv[i, j].astype(F32) for j in range(3)] for i in range(2)]
    for t in range(26):
        row, col = place(t * 128, 2 * LEV, 128)
        tile = xf[:, LEAD + t * 128 : LEAD + t * 128 + 128]
        left, right = sides[0][1], sides[1][1]
        if t < 5:
            above = row < HALO
            tile = jnp.where(above, band_recv[0, :, t * 128 : t * 128 + 128].astype(F32), tile)
            left = jnp.where(above, sides[0][0], left)
            right = jnp.where(above, sides[1][0], right)
        if t >= 21:
            below = row >= HALO + ROWS
            tile = jnp.where(below, band_recv[1, :, (t - 21) * 128 : (t - 20) * 128].astype(F32), tile)
            left = jnp.where(below, sides[0][2], left)
            right = jnp.where(below, sides[1][2], right)
        tile = jnp.where(col < HALO, left, tile)
        tile = jnp.where(col >= HALO + COLS, right, tile)
        if t < 5 or t >= 21:
            tile = jnp.where((row >= row_low) & (row < row_high), tile, 0.0)
        xf[:, LEAD + t * 128 : LEAD + t * 128 + 128] = tile
        if PRED_FIRST <= t < PRED_FIRST + PRED_TILES:
            target_tiles[t - PRED_FIRST] = tile[LEV:]

    for k, shift in enumerate(SHIFTS):
        xc[k * LEV : (k + 1) * LEV, 128:3200] = xf[0:LEV, LEAD + 128 + shift : LEAD + 3200 + shift].astype(BF16)

    def forward(i, carry):
        start = pl.multiple_of(128 + i * 256, 128)
        lanes = pl.ds(start, 256)
        hidden = jnp.dot(w_in[...], xc[:, lanes], preferred_element_type=F32)
        hidden += jnp.concatenate([bias[...], bias[...]], axis=1)
        pre[:, lanes] = hidden
        lane = lax.broadcasted_iota(jnp.int32, (C, 256), 1) + start
        inside = (lane >= low_lane) & (lane < high_lane)
        value = jnp.where(inside, hidden * jax.nn.sigmoid(hidden), 0.0).astype(BF16)
        act[:, lanes] = value
        taps[:, lanes] = jnp.dot(
            wout16[...].reshape(TAPS, C), value, preferred_element_type=F32
        )
        return carry

    low_lane = jnp.where(me_a == 0, HALO * PITCH, 0)
    high_lane = jnp.where(me_a == lats - 1, (HALO + ROWS) * PITCH, FLAT)
    lax.fori_loop(0, 12, forward, 0)

    for t in range(0, PRED_TILES, 2):
        first = (PRED_FIRST + t) * 128
        total = xf[0:LEV, LEAD + first : LEAD + first + 256]
        for k, shift in enumerate(SHIFTS):
            total += taps[k * LEV : (k + 1) * LEV, first + shift : first + shift + 256]
        for u in (t, t + 1):
            pred_send[u % members, u // members] = total[:, (u - t) * 128 : (u - t + 1) * 128].astype(BF16)

    for dz, h in group_m:
        device = at(dz, h, 0, 0)
        send(pred_send.at[device[0]], pred_recv.at[me_m], 2, device)
    pred_recv[me_m] = pred_send[me_m]

    def own_slopes(i, carry):
        start = pl.multiple_of(384 + i * 256, 128)
        lanes = pl.ds(start, 256)
        hidden = pre[:, lanes]
        gate = jax.nn.sigmoid(hidden)
        pre[:, lanes] = gate * (1.0 + hidden * (1.0 - gate))
        row, col = place(0, C, 256)
        lane = lax.broadcasted_iota(jnp.int32, (C, 256), 1).astype(F32) + start.astype(F32)
        row = jnp.floor((lane + 0.5) * (1.0 / PITCH))
        col = lane - PITCH * row
        own = (row >= HALO) & (row < HALO + ROWS) & (col >= HALO) & (col < HALO + COLS)
        act_own[:, lanes] = jnp.where(own, act[:, lanes].astype(F32), 0.0).astype(BF16)
        return carry

    lax.fori_loop(0, 10, own_slopes, 0)
    wait_recv(pred_recv.at[pl.ds(0, members - 1)], 2)

    coupling = (1.0 - 0.05 / members) / (members - 1)

    def slope(d):
        return d * lax.rsqrt(d * d + 0.25)

    for u in range(share):
        everyone = pred_recv[:, u].astype(F32)
        wanted = target_tiles[me_m + u * members]
        for half in range(2):
            own = everyone[:, half * 8 : half * 8 + 8]
            spread = jnp.zeros_like(own)
            for d in range(1, members // 2 + 1):
                term = slope(own - jnp.concatenate([own[d:], own[:d]], axis=0))
                spread += term
                if 2 * d != members:
                    spread -= jnp.concatenate([term[members - d :], term[: members - d]], axis=0)
            value = slope(own - wanted[None, half * 8 : half * 8 + 8]) - coupling * spread
            field[:, half * 8 : half * 8 + 8, :] = value
        grad_send[:, u] = field[...].astype(BF16)

    for dz, h in group_m:
        device = at(dz, h, 0, 0)
        send(grad_send.at[device[0]], grad_recv.at[me_m], 3, device)
    grad_recv[me_m] = grad_send[me_m]
    wait_recv(grad_recv.at[pl.ds(0, members - 1)], 3)

    for u in range(PRED_TILES):
        t = PRED_FIRST + u
        row, col = place(t * 128, LEV, 128)
        inside = (row >= row_low) & (row < row_high) & (col >= HALO - 2) & (col < HALO + COLS + 2)
        tile = grad_recv[u % members, u // members].astype(F32)
        gp[:, t * 128 : t * 128 + 128] = jnp.where(inside, tile, 0.0)
    for k, shift in enumerate(SHIFTS):
        gc[k * LEV : (k + 1) * LEV, 384:2944] = gp[:, 384 - shift : 2944 - shift].astype(BF16)

    contract_lanes = (((1,), (1,)), ((), ()))
    out_part = lax.dot_general(
        gc[:, 512:2816], act_own[:, 512:2816], contract_lanes, preferred_element_type=F32
    )
    part_sum[0, 0:PART] = out_part.reshape(PART, 8, C)
    part_sum[0, PART:] = jnp.zeros((quads * chunk - PART, 8, C), F32)
    for h, da in group_q:
        device = at(0, h, da, 0)
        slot = (device[0] % 2) * lats + device[1]
        send(part_sum.at[0, pl.ds(slot * chunk, chunk)], part_recv.at[0, me_q], 4, device)

    def backward(i, carry):
        start = pl.multiple_of(384 + i * 256, 128)
        lanes = pl.ds(start, 256)
        value = jnp.dot(w_out_t[...], gc[:, lanes], preferred_element_type=F32) * pre[:, lanes]
        lane = lax.broadcasted_iota(jnp.int32, (C, 256), 1)
        inside = (lane + start >= low_lane) & (lane + start < high_lane)
        value = jnp.where(inside, value, 0.0)
        spread = lane.astype(F32) + start.astype(F32)
        row = jnp.floor((spread + 0.5) * (1.0 / PITCH))
        col = spread - PITCH * row
        own = (row >= HALO) & (row < HALO + ROWS) & (col >= HALO) & (col < HALO + COLS)
        gh[:, lanes] = jnp.where(own, value, 0.0).astype(BF16)
        taps[:, lanes] = jnp.dot(w_in_t[...], value.astype(BF16), preferred_element_type=F32)
        return carry

    lax.fori_loop(0, 10, backward, 0)
    in_part = lax.dot_general(
        xc[:, 512:2816], gh[:, 512:2816], contract_lanes, preferred_element_type=F32
    )
    part_sum[1, 0:PART] = in_part.reshape(PART, 8, C)
    part_sum[1, PART:] = jnp.zeros((quads * chunk - PART, 8, C), F32)
    for h, da in group_q:
        device = at(0, h, da, 0)
        slot = (device[0] % 2) * lats + device[1]
        send(part_sum.at[1, pl.ds(slot * chunk, chunk)], part_recv.at[1, me_q], 5, device)
    for p in range(2):
        part_recv[p, me_q] = part_sum[p, pl.ds(me_q * chunk, chunk)]

    for r in range(ROWS):
        start = PITCH * (r + HALO) + HALO
        total = gp[:, start : start + COLS]
        for k, shift in enumerate(SHIFTS):
            total += taps[k * LEV : (k + 1) * LEV, start - shift : start - shift + COLS]
        field[:, r, :] = total
    store = pltpu.make_async_copy(field, field_hbm.at[0], load_sem.at[0])
    store.start()

    wait_recv(part_recv.at[0, pl.ds(0, quads - 1)], 4)
    wait_recv(part_recv.at[1, pl.ds(0, quads - 1)], 5)
    for p in range(2):
        total = part_recv[p, 0]
        for q in range(1, quads):
            total += part_recv[p, q]
        lon_recv[me_o, pl.ds(p * chunk, chunk)] = total
    for d in group_o:
        send(lon_recv.at[me_o], lon_recv.at[me_o], 6, at(0, 0, 0, d))
    wait_recv(lon_recv.at[pl.ds(0, lons - 1)], 6)
    total = lon_recv[0]
    for i in range(1, lons):
        total += lon_recv[i]
    mem_recv[me_z] = total
    for d in group_z:
        send(mem_recv.at[me_z], mem_recv.at[me_z], 7, at(d, 0, 0, 0))
    wait_recv(mem_recv.at[pl.ds(0, zs - 1)], 7)
    total = mem_recv[0]
    for i in range(1, zs):
        total += mem_recv[i]
    all_recv[me_q] = total * (1.0 / math.sqrt(members * lats * lons * ROWS * COLS))
    for h, da in group_q:
        send(all_recv.at[me_q], all_recv.at[me_q], 8, at(0, h, da, 0))
    wait_recv(all_recv.at[pl.ds(0, quads - 1)], 8)

    for t in range(PART):
        k, half = t // 2, t % 2
        gout_ref[k, half * 8 : half * 8 + 8, :] = all_recv[t // chunk, t % chunk]
    for k in range(9):
        pair = [all_recv[t // chunk, chunk + t % chunk] for t in (2 * k, 2 * k + 1)]
        gin_ref[k] = jnp.concatenate(pair, axis=0).T

    store.wait()
    wait_send(side_recv, 0)
    wait_send(band_recv, 1)
    wait_send(pred_recv.at[pl.ds(0, members - 1)], 2)
    wait_send(grad_recv.at[pl.ds(0, members - 1)], 3)
    wait_send(part_recv.at[0, pl.ds(0, quads - 1)], 4)
    wait_send(part_recv.at[1, pl.ds(0, quads - 1)], 5)
    wait_send(lon_recv.at[pl.ds(0, lons - 1)], 6)
    wait_send(mem_recv.at[pl.ds(0, zs - 1)], 7)
    wait_send(all_recv.at[pl.ds(0, quads - 1)], 8)


def shards(sizes, inputs, target, conv_in, bias_in, conv_out):
    members, lats, lons = sizes
    quads = 2 * lats
    share = -(-PRED_TILES // members)
    chunk = -(-PART // quads)
    wide = FLAT + LEAD + 128
    return pl.pallas_call(
        functools.partial(kernel, sizes),
        out_shape=(
            jax.ShapeDtypeStruct((1, LEV, ROWS, COLS), F32),
            jax.ShapeDtypeStruct((9, C, LEV), F32),
            jax.ShapeDtypeStruct((9, LEV, C), F32),
        ),
        in_specs=[
            pl.BlockSpec(memory_space=pl.ANY),
            pl.BlockSpec(memory_space=pl.ANY),
            pl.BlockSpec(memory_space=pl.ANY),
            pl.BlockSpec(memory_space=pltpu.VMEM),
            pl.BlockSpec(memory_space=pl.ANY),
        ],
        out_specs=(
            pl.BlockSpec(memory_space=pl.ANY),
            pl.BlockSpec(memory_space=pltpu.VMEM),
            pl.BlockSpec(memory_space=pltpu.VMEM),
        ),
        scratch_shapes=[
            pltpu.VMEM((LEV, ROWS, COLS), BF16),
            pltpu.VMEM((LEV, ROWS, COLS), BF16),
            pltpu.VMEM((9, C, LEV), BF16),
            pltpu.VMEM((9, LEV, C), BF16),
            pltpu.VMEM((2 * LEV, ROWS, COLS), F32),
            pltpu.VMEM((2 * LEV, wide), F32),
            pltpu.VMEM((C, TAPS), BF16),
            pltpu.VMEM((TAPS, C), BF16),
            pltpu.VMEM((C, TAPS), BF16),
            pltpu.VMEM((C, C), F32),
            pltpu.VMEM((2, 2 * LEV, 128), BF16),
            pltpu.VMEM((2, 2 * LEV, 640), BF16),
            pltpu.VMEM((2, 3, 2 * LEV, 128), BF16),
            pltpu.VMEM((2, 2 * LEV, 640), BF16),
            pltpu.VMEM((TAPS, FLAT), BF16),
            pltpu.VMEM((C, FLAT), F32),
            pltpu.VMEM((C, FLAT), BF16),
            pltpu.VMEM((C, FLAT), BF16),
            pltpu.VMEM((TAPS, FLAT), F32),
            pltpu.VMEM((members, share, LEV, 128), BF16),
            pltpu.VMEM((members, share, LEV, 128), BF16),
            pltpu.VMEM((members * share, LEV, 128), F32),
            pltpu.VMEM((members, share, LEV, 128), BF16),
            pltpu.VMEM((members, share, LEV, 128), BF16),
            pltpu.VMEM((LEV, FLAT), F32),
            pltpu.VMEM((TAPS, FLAT), BF16),
            pltpu.VMEM((C, FLAT), BF16),
            pltpu.VMEM((LEV, ROWS, COLS), F32),
            pltpu.VMEM((2, quads * chunk, 8, C), F32),
            pltpu.VMEM((2, quads, chunk, 8, C), F32),
            pltpu.VMEM((lons, 2 * chunk, 8, C), F32),
            pltpu.VMEM((members // 2, 2 * chunk, 8, C), F32),
            pltpu.VMEM((quads, 2 * chunk, 8, C), F32),
            pltpu.SemaphoreType.DMA((4,)),
            pltpu.SemaphoreType.DMA((9,)),
            pltpu.SemaphoreType.DMA((9,)),
        ],
        compiler_params=pltpu.CompilerParams(
            collective_id=0, has_side_effects=True, vmem_limit_bytes=40 * 1024 * 1024
        ),
        name="downscaling_step",
    )(inputs, target, conv_in, bias_in.reshape(1, C), conv_out)


def solution(mesh):
    sizes = tuple(mesh.shape[axis] for axis in ("member", "lat", "lon"))
    in_specs = (P("member", None, "lat", "lon"), P(None, "lat", "lon"), P(), P(), P())
    out_specs = (P("member", None, "lat", "lon"), P(), P())
    return jax.shard_map(
        functools.partial(shards, sizes),
        mesh=mesh,
        in_specs=in_specs,
        out_specs=out_specs,
        check_vma=False,
    )
```

```python
import functools
import math

import jax
import jax.numpy as jnp
from jax import lax
from jax.experimental import pallas as pl
from jax.experimental.pallas import tpu as pltpu
from jax.sharding import PartitionSpec as P

MESH = pl.DeviceIdType.MESH
F32 = jnp.float32
BF16 = jnp.bfloat16

LEV = 16
C = 128
ROWS = 16
COLS = 128
HALO = 4
PITCH = COLS + 2 * HALO
FLAT = 26 * 128
LEAD = 128
OFFSETS = [(di, dj) for di in (-1, 0, 1) for dj in (-1, 0, 1)]
SHIFTS = [di * PITCH + dj for di, dj in OFFSETS]
PRED_FIRST = 2
PRED_TILES = 22
TAPS = 9 * LEV
PART = TAPS // 8
VMEM_LIMIT = 40 * 1024 * 1024


def ring_order(count):
    return sorted(range(count), key=lambda d: (-min(d, count - d), d))


def kernel(
    sizes,
    x_hbm,
    t_hbm,
    w_in_hbm,
    bias_ref,
    w_out_hbm,
    field,
    sums_ref,
    x16,
    t16,
    w_in_t,
    w_out,
    bias16,
    rows32,
    xf,
    w_in,
    w_out_t,
    bias,
    masks,
    side_send,
    band_send,
    side_recv,
    band_recv,
    xc,
    pre,
    act,
    act_own,
    taps,
    pred_send,
    pred_recv,
    target_tiles,
    grads,
    grad_send,
    grad_recv,
    gp,
    gc,
    gh,
    gh_own,
    by_row,
    part_sum,
    part_recv,
    lon_recv,
    mem_recv,
    all_recv,
    load_sem,
    send_sem,
    recv_sem,
):
    members, lats, lons = sizes
    zs = members // 2
    quads = 2 * lats
    share = -(-PRED_TILES // members)
    chunk = -(-PART // quads)
    me_m = lax.axis_index("member")
    me_a = lax.axis_index("lat")
    me_o = lax.axis_index("lon")
    me_z = me_m // 2
    me_h = me_m % 2
    me_q = me_h * lats + me_a

    loads = [
        pltpu.make_async_copy(src, dst, load_sem.at[i])
        for i, (src, dst) in enumerate(
            (
                (x_hbm.at[0], x16),
                (t_hbm, t16),
                (w_in_hbm, w_in_t),
                (w_out_hbm, w_out),
                (bias_ref, bias16),
            )
        )
    ]
    for load in loads:
        load.start()

    def at(dm_z, dm_h, da, do):
        return (
            ((me_z + dm_z) % zs) * 2 + (me_h + dm_h) % 2,
            (me_a + da + lats) % lats,
            (me_o + do + lons) % lons,
        )

    halo = [(da, do) for da, do in ((-1, -1), (-1, 1), (1, -1), (1, 1), (0, -1), (0, 1), (-1, 0), (1, 0))]
    group_m = [(dz, h) for dz in ring_order(zs) for h in (1, 0) if dz or h]
    group_q = [(h, da) for h in (1, 0) for da in ring_order(lats) if h or da]
    group_o = [d for d in ring_order(lons) if d]
    group_z = [d for d in ring_order(zs) if d]

    barrier = pltpu.get_barrier_semaphore()
    greet = [at(dz, h, 0, 0) for dz, h in group_m]
    greet += [at(0, 0, 0, d) for d in group_o]
    greet += [at(0, h, da, 0) for h, da in group_q]
    greet += [at(0, 0, da, do) for da, do in halo]
    for device in greet:
        pl.semaphore_signal(barrier, inc=1, device_id=device, device_id_type=MESH)

    loads[0].wait()
    loads[1].wait()
    rows32[0:LEV] = x16[...].astype(F32)
    rows32[LEV:] = t16[...].astype(F32)
    for r in range(ROWS):
        start = LEAD + PITCH * (r + HALO) + HALO
        xf[:, start : start + COLS] = rows32[:, r, :]

    def place(first, height, width):
        lane = lax.broadcasted_iota(jnp.int32, (height, width), 1).astype(F32) + float(first)
        row = jnp.floor((lane + 0.5) * (1.0 / PITCH))
        return row, lane - PITCH * row

    left_edge = jnp.zeros((2 * LEV, 128), F32)
    right_edge = jnp.zeros((2 * LEV, 128), F32)
    for t in range(4, 22):
        row, col = place(t * 128, 2 * LEV, 128)
        here = (row >= HALO) & (row < HALO + ROWS)
        tile = xf[:, LEAD + t * 128 : LEAD + t * 128 + 128]
        left_edge += jnp.where(here & (col >= HALO) & (col < 2 * HALO), tile, 0.0)
        right_edge += jnp.where(here & (col >= COLS) & (col < COLS + HALO), tile, 0.0)
    side_send[0] = right_edge.astype(BF16)
    side_send[1] = left_edge.astype(BF16)
    band_send[0] = xf[:, LEAD + 17 * 128 : LEAD + 22 * 128].astype(BF16)
    band_send[1] = xf[:, LEAD + 4 * 128 : LEAD + 9 * 128].astype(BF16)

    pl.semaphore_wait(barrier, len(greet))

    def send(src, dst, phase, device):
        copy = pltpu.make_async_remote_copy(
            src_ref=src,
            dst_ref=dst,
            send_sem=send_sem.at[phase],
            recv_sem=recv_sem.at[phase],
            device_id=device,
            device_id_type=MESH,
        )
        copy.start()

    def wait_recv(ref, phase):
        pltpu.make_async_remote_copy(
            src_ref=ref,
            dst_ref=ref,
            send_sem=send_sem.at[phase],
            recv_sem=recv_sem.at[phase],
            device_id=(me_m, me_a, (me_o + 1) % lons),
            device_id_type=MESH,
        ).wait_recv()

    def wait_send(ref, phase):
        pltpu.make_async_remote_copy(
            src_ref=ref,
            dst_ref=ref,
            send_sem=send_sem.at[phase],
            recv_sem=recv_sem.at[phase],
            device_id=(me_m, me_a, (me_o + 1) % lons),
            device_id_type=MESH,
        ).wait_send()

    for da in (-1, 1, 0):
        send(side_send.at[0], side_recv.at[0, 1 - da], 0, at(0, 0, da, 1))
        send(side_send.at[1], side_recv.at[1, 1 - da], 0, at(0, 0, da, -1))
    send(band_send.at[0], band_recv.at[0], 1, at(0, 0, 1, 0))
    send(band_send.at[1], band_recv.at[1], 1, at(0, 0, -1, 0))

    for load in loads[2:]:
        load.wait()
    w_in[...] = w_in_t[...].astype(F32).T.astype(BF16)
    w_out_t[...] = w_out[...].astype(F32).T.astype(BF16)
    bias[...] = jnp.broadcast_to(bias16[...], (C, C)).T
    taps[:, 0:128] = jnp.zeros((TAPS, 128), F32)
    taps[:, FLAT - 128 : FLAT] = jnp.zeros((TAPS, 128), F32)
    xf[:, 0:LEAD] = jnp.zeros((2 * LEV, LEAD), F32)
    xf[:, LEAD + FLAT :] = jnp.zeros((2 * LEV, 128), F32)
    gp[:, 0 : PRED_FIRST * 128] = jnp.zeros((LEV, PRED_FIRST * 128), F32)
    gp[:, (PRED_FIRST + PRED_TILES) * 128 :] = jnp.zeros((LEV, PRED_FIRST * 128), F32)
    spare = members * share - PRED_TILES
    for u in range(PRED_TILES, PRED_TILES + spare):
        target_tiles[u] = jnp.zeros((LEV, 128), F32)
        pred_send[u % members, u // members] = jnp.zeros((LEV, 128), BF16)
    for p in range(2):
        part_sum[p, PART:] = jnp.zeros((quads * chunk - PART, 8, C), F32)
    row_low = jnp.where(me_a == 0, HALO, 0).astype(F32)
    row_high = jnp.where(me_a == lats - 1, HALO + ROWS, ROWS + 2 * HALO).astype(F32)
    row, col = place(0, 8, FLAT)
    masks[0] = jnp.where((row >= row_low) & (row < row_high), 1.0, 0.0)
    masks[1] = jnp.where(
        (row >= HALO) & (row < HALO + ROWS) & (col >= HALO) & (col < HALO + COLS), 1.0, 0.0
    )

    wait_recv(side_recv, 0)
    wait_recv(band_recv, 1)

    sides = [[side_recv[i, j].astype(F32) for j in range(3)] for i in range(2)]
    for t in range(26):
        row, col = place(t * 128, 2 * LEV, 128)
        tile = xf[:, LEAD + t * 128 : LEAD + t * 128 + 128]
        left, right = sides[0][1], sides[1][1]
        if t < 5:
            above = row < HALO
            tile = jnp.where(above, band_recv[0, :, t * 128 : t * 128 + 128].astype(F32), tile)
            left = jnp.where(above, sides[0][0], left)
            right = jnp.where(above, sides[1][0], right)
        if t >= 21:
            below = row >= HALO + ROWS
            tile = jnp.where(below, band_recv[1, :, (t - 21) * 128 : (t - 20) * 128].astype(F32), tile)
            left = jnp.where(below, sides[0][2], left)
            right = jnp.where(below, sides[1][2], right)
        tile = jnp.where(col < HALO, left, tile)
        tile = jnp.where(col >= HALO + COLS, right, tile)
        if t < 5 or t >= 21:
            tile = jnp.where((row >= row_low) & (row < row_high), tile, 0.0)
        xf[:, LEAD + t * 128 : LEAD + t * 128 + 128] = tile
        if PRED_FIRST <= t < PRED_FIRST + PRED_TILES:
            target_tiles[t - PRED_FIRST] = tile[LEV:]

    for k, shift in enumerate(SHIFTS):
        xc[k * LEV : (k + 1) * LEV, 128:3200] = xf[0:LEV, LEAD + 128 + shift : LEAD + 3200 + shift].astype(BF16)

    def mask(which, first, last):
        return masks[which, 0:1, first:last] > 0.5

    hidden = jnp.dot(w_in[...], xc[:, 128:3200], preferred_element_type=F32)
    hidden += jnp.concatenate([bias[...]] * 24, axis=1)
    pre[:, 128:3200] = hidden
    value = jnp.where(mask(0, 128, 3200), hidden * jax.nn.sigmoid(hidden), 0.0).astype(BF16)
    act[:, 128:3200] = value
    taps[:, 128:3200] = jnp.dot(w_out[...], value, preferred_element_type=F32)

    for t in range(0, PRED_TILES, 2):
        first = (PRED_FIRST + t) * 128
        total = xf[0:LEV, LEAD + first : LEAD + first + 256]
        for k, shift in enumerate(SHIFTS):
            total += taps[k * LEV : (k + 1) * LEV, first + shift : first + shift + 256]
        for u in (t, t + 1):
            pred_send[u % members, u // members] = total[:, (u - t) * 128 : (u - t + 1) * 128].astype(BF16)

    for dz, h in group_m:
        device = at(dz, h, 0, 0)
        send(pred_send.at[device[0]], pred_recv.at[me_m], 2, device)
    pred_recv[me_m] = pred_send[me_m]

    hidden = pre[:, 384:2944]
    gate = jax.nn.sigmoid(hidden)
    pre[:, 384:2944] = gate * (1.0 + hidden * (1.0 - gate))
    act_own[:, 384:2944] = jnp.where(
        mask(1, 384, 2944), act[:, 384:2944].astype(F32), 0.0
    ).astype(BF16)
    wait_recv(pred_recv.at[pl.ds(0, members - 1)], 2)

    coupling = (1.0 - 0.05 / members) / (members - 1)

    def slope(d):
        return d * lax.rsqrt(d * d + 0.25)

    for u in range(share):
        everyone = pred_recv[:, u].astype(F32)
        wanted = target_tiles[me_m + u * members]
        for half in range(2):
            own = everyone[:, half * 8 : half * 8 + 8]
            spread = jnp.zeros_like(own)
            for d in range(1, members // 2 + 1):
                term = slope(own - jnp.concatenate([own[d:], own[:d]], axis=0))
                spread += term
                if 2 * d != members:
                    spread -= jnp.concatenate([term[members - d :], term[: members - d]], axis=0)
            value = slope(own - wanted[None, half * 8 : half * 8 + 8]) - coupling * spread
            grads[:, half * 8 : half * 8 + 8, :] = value
        grad_send[:, u] = grads[...].astype(BF16)

    for dz, h in group_m:
        device = at(dz, h, 0, 0)
        send(grad_send.at[device[0]], grad_recv.at[me_m], 3, device)
    grad_recv[me_m] = grad_send[me_m]
    wait_recv(grad_recv.at[pl.ds(0, members - 1)], 3)

    for u in range(PRED_TILES):
        t = PRED_FIRST + u
        row, col = place(t * 128, LEV, 128)
        inside = (row >= row_low) & (row < row_high) & (col >= HALO - 2) & (col < HALO + COLS + 2)
        tile = grad_recv[u % members, u // members].astype(F32)
        gp[:, t * 128 : t * 128 + 128] = jnp.where(inside, tile, 0.0)
    for k, shift in enumerate(SHIFTS):
        gc[k * LEV : (k + 1) * LEV, 384:2944] = gp[:, 384 - shift : 2944 - shift].astype(BF16)

    contract_lanes = (((1,), (1,)), ((), ()))
    out_part = lax.dot_general(
        gc[:, 512:2816], act_own[:, 512:2816], contract_lanes, preferred_element_type=F32
    )
    part_sum[0, 0:PART] = out_part.reshape(PART, 8, C)
    for h, da in group_q:
        device = at(0, h, da, 0)
        slot = (device[0] % 2) * lats + device[1]
        send(part_sum.at[0, pl.ds(slot * chunk, chunk)], part_recv.at[0, me_q], 4, device)

    value = jnp.dot(w_out_t[...], gc[:, 384:2944], preferred_element_type=F32) * pre[:, 384:2944]
    gh_own[:, 384:2944] = jnp.where(mask(1, 384, 2944), value, 0.0).astype(BF16)
    gh[:, 384:2944] = jnp.where(mask(0, 384, 2944), value, 0.0).astype(BF16)
    in_part = lax.dot_general(
        xc[:, 512:2816], gh_own[:, 512:2816], contract_lanes, preferred_element_type=F32
    )
    part_sum[1, 0:PART] = in_part.reshape(PART, 8, C)
    for h, da in group_q:
        device = at(0, h, da, 0)
        slot = (device[0] % 2) * lats + device[1]
        send(part_sum.at[1, pl.ds(slot * chunk, chunk)], part_recv.at[1, me_q], 5, device)
    for p in range(2):
        part_recv[p, me_q] = part_sum[p, pl.ds(me_q * chunk, chunk)]

    def total_of(ref, count):
        total = ref[0]
        for i in range(1, count):
            total += ref[i]
        return total

    def to_lons(p, phase):
        for d in group_o:
            send(lon_recv.at[p, me_o], lon_recv.at[p, me_o], phase, at(0, 0, 0, d))

    def to_zs(p, phase):
        for d in group_z:
            send(mem_recv.at[p, me_z], mem_recv.at[p, me_z], phase, at(d, 0, 0, 0))

    wait_recv(part_recv.at[0, pl.ds(0, quads - 1)], 4)
    lon_recv[0, me_o] = total_of(part_recv.at[0], quads)
    to_lons(0, 6)

    taps[:, 384:2944] = jnp.dot(w_in_t[...], gh[:, 384:2944], preferred_element_type=F32)
    for r in range(ROWS):
        start = PITCH * (r + HALO) + HALO
        total = gp[:, start : start + COLS]
        for k, shift in enumerate(SHIFTS):
            total += taps[k * LEV : (k + 1) * LEV, start - shift : start - shift + COLS]
        by_row[r] = total
    for level in range(LEV):
        field[level] = by_row[:, level, :]

    wait_recv(part_recv.at[1, pl.ds(0, quads - 1)], 5)
    mem_recv[1, me_z] = total_of(part_recv.at[1], quads)
    to_zs(1, 7)
    wait_recv(lon_recv.at[0, pl.ds(0, lons - 1)], 6)
    mem_recv[0, me_z] = total_of(lon_recv.at[0], lons)
    to_zs(0, 8)
    wait_recv(mem_recv.at[1, pl.ds(0, zs - 1)], 7)
    lon_recv[1, me_o] = total_of(mem_recv.at[1], zs)
    to_lons(1, 9)
    scale = 1.0 / math.sqrt(members * lats * lons * ROWS * COLS)
    wait_recv(mem_recv.at[0, pl.ds(0, zs - 1)], 8)
    all_recv[0, me_q] = total_of(mem_recv.at[0], zs) * scale
    for h, da in group_q:
        send(all_recv.at[0, me_q], all_recv.at[0, me_q], 10, at(0, h, da, 0))
    wait_recv(lon_recv.at[1, pl.ds(0, lons - 1)], 9)
    all_recv[1, me_q] = total_of(lon_recv.at[1], lons) * scale
    for h, da in group_q:
        send(all_recv.at[1, me_q], all_recv.at[1, me_q], 11, at(0, h, da, 0))

    wait_send(side_recv, 0)
    wait_send(band_recv, 1)
    wait_send(pred_recv.at[pl.ds(0, members - 1)], 2)
    wait_send(grad_recv.at[pl.ds(0, members - 1)], 3)
    for p in range(2):
        wait_send(part_recv.at[p, pl.ds(0, quads - 1)], 4 + p)
        wait_send(lon_recv.at[p, pl.ds(0, lons - 1)], 6 + 3 * p)
        wait_send(mem_recv.at[p, pl.ds(0, zs - 1)], 8 - p)
    for p in range(2):
        wait_recv(all_recv.at[p, pl.ds(0, quads - 1)], 10 + p)
        for t in range(PART):
            sums_ref[p, t] = all_recv[p, t // chunk, t % chunk]
    for p in range(2):
        wait_send(all_recv.at[p, pl.ds(0, quads - 1)], 10 + p)


def write_out(field, sums, field_out, gin_out, gout_out, sem):
    copies = [
        pltpu.make_async_copy(src, dst, sem.at[i])
        for i, (src, dst) in enumerate(
            ((field, field_out.at[0]), (sums.at[1], gin_out), (sums.at[0], gout_out))
        )
    ]
    for copy in copies:
        copy.start()
    for copy in copies:
        copy.wait()


def shards(sizes, inputs, target, conv_in, bias_in, conv_out):
    members, lats, lons = sizes
    quads = 2 * lats
    share = -(-PRED_TILES // members)
    chunk = -(-PART // quads)
    wide = FLAT + LEAD + 128
    anywhere = pl.BlockSpec(memory_space=pl.ANY)
    near = pl.BlockSpec(memory_space=pltpu.VMEM)
    field, sums = pl.pallas_call(
        functools.partial(kernel, sizes),
        out_shape=(
            pltpu.VMEM((LEV, ROWS, COLS), F32),
            pltpu.VMEM((2, PART, 8, C), F32),
        ),
        in_specs=[pl.BlockSpec(memory_space=pltpu.HBM)] * 5,
        out_specs=(near, near),
        scratch_shapes=[
            pltpu.VMEM((LEV, ROWS, COLS), BF16),
            pltpu.VMEM((LEV, ROWS, COLS), BF16),
            pltpu.VMEM((TAPS, C), BF16),
            pltpu.VMEM((TAPS, C), BF16),
            pltpu.VMEM((1, C), F32),
            pltpu.VMEM((2 * LEV, ROWS, COLS), F32),
            pltpu.VMEM((2 * LEV, wide), F32),
            pltpu.VMEM((C, TAPS), BF16),
            pltpu.VMEM((C, TAPS), BF16),
            pltpu.VMEM((C, C), F32),
            pltpu.VMEM((2, 8, FLAT), F32),
            pltpu.VMEM((2, 2 * LEV, 128), BF16),
            pltpu.VMEM((2, 2 * LEV, 640), BF16),
            pltpu.VMEM((2, 3, 2 * LEV, 128), BF16),
            pltpu.VMEM((2, 2 * LEV, 640), BF16),
            pltpu.VMEM((TAPS, FLAT), BF16),
            pltpu.VMEM((C, FLAT), F32),
            pltpu.VMEM((C, FLAT), BF16),
            pltpu.VMEM((C, FLAT), BF16),
            pltpu.VMEM((TAPS, FLAT), F32),
            pltpu.VMEM((members, share, LEV, 128), BF16),
            pltpu.VMEM((members, share, LEV, 128), BF16),
            pltpu.VMEM((members * share, LEV, 128), F32),
            pltpu.VMEM((members, LEV, 128), F32),
            pltpu.VMEM((members, share, LEV, 128), BF16),
            pltpu.VMEM((members, share, LEV, 128), BF16),
            pltpu.VMEM((LEV, FLAT), F32),
            pltpu.VMEM((TAPS, FLAT), BF16),
            pltpu.VMEM((C, FLAT), BF16),
            pltpu.VMEM((C, FLAT), BF16),
            pltpu.VMEM((ROWS, LEV, COLS), F32),
            pltpu.VMEM((2, quads * chunk, 8, C), F32),
            pltpu.VMEM((2, quads, chunk, 8, C), F32),
            pltpu.VMEM((2, lons, chunk, 8, C), F32),
            pltpu.VMEM((2, members // 2, chunk, 8, C), F32),
            pltpu.VMEM((2, quads, chunk, 8, C), F32),
            pltpu.SemaphoreType.DMA((5,)),
            pltpu.SemaphoreType.DMA((12,)),
            pltpu.SemaphoreType.DMA((12,)),
        ],
        compiler_params=pltpu.CompilerParams(
            collective_id=0, has_side_effects=True, vmem_limit_bytes=VMEM_LIMIT
        ),
        name="downscaling_step",
    )(
        *(
            pltpu.with_memory_space_constraint(operand, pltpu.HBM)
            for operand in (
                inputs,
                target,
                conv_in.transpose(0, 2, 1).reshape(TAPS, C),
                bias_in.reshape(1, C),
                conv_out.reshape(TAPS, C),
            )
        )
    )
    field, gin, gout = pl.pallas_call(
        write_out,
        out_shape=(
            jax.ShapeDtypeStruct((1, LEV, ROWS, COLS), F32),
            jax.ShapeDtypeStruct((PART, 8, C), F32),
            jax.ShapeDtypeStruct((PART, 8, C), F32),
        ),
        in_specs=[near] * 2,
        out_specs=(anywhere,) * 3,
        scratch_shapes=[pltpu.SemaphoreType.DMA((3,))],
        compiler_params=pltpu.CompilerParams(vmem_limit_bytes=1024 * 1024),
        name="write_out",
    )(field, sums)
    return field, gin.reshape(9, LEV, C).transpose(0, 2, 1), gout.reshape(9, LEV, C)


def solution(mesh):
    sizes = tuple(mesh.shape[axis] for axis in ("member", "lat", "lon"))
    in_specs = (P("member", None, "lat", "lon"), P(None, "lat", "lon"), P(), P(), P())
    out_specs = (P("member", None, "lat", "lon"), P(), P())
    return jax.shard_map(
        functools.partial(shards, sizes),
        mesh=mesh,
        in_specs=in_specs,
        out_specs=out_specs,
        check_vma=False,
    )
```

```python
import functools
import math

import jax
import jax.numpy as jnp
from jax import lax
from jax.experimental import pallas as pl
from jax.experimental.pallas import tpu as pltpu
from jax.sharding import PartitionSpec as P

MESH = pl.DeviceIdType.MESH
F32 = jnp.float32
BF16 = jnp.bfloat16

LEV = 16
C = 128
ROWS = 16
COLS = 128
HALO = 4
PITCH = COLS + 2 * HALO
FLAT = 26 * 128
LEAD = 128
OFFSETS = [(di, dj) for di in (-1, 0, 1) for dj in (-1, 0, 1)]
SHIFTS = [di * PITCH + dj for di, dj in OFFSETS]
PRED_FIRST = 2
PRED_TILES = 22
TAPS = 9 * LEV
PART = TAPS // 8
VMEM_LIMIT = 40 * 1024 * 1024


def ring_order(count):
    return sorted(range(count), key=lambda d: (-min(d, count - d), d))


def kernel(
    sizes,
    x_hbm,
    t_hbm,
    w_in_hbm,
    bias_ref,
    w_out_hbm,
    field,
    sums_ref,
    x16,
    t16,
    w_in_t,
    w_out,
    bias16,
    rows32,
    xf,
    w_in,
    w_out_t,
    bias,
    masks,
    side_send,
    band_send,
    side_recv,
    band_recv,
    xc,
    pre,
    act,
    act_own,
    taps,
    pred_send,
    pred_recv,
    target_tiles,
    grads,
    grad_send,
    grad_recv,
    gp,
    gc,
    gh,
    gh_own,
    by_row,
    part_sum,
    part_recv,
    lon_recv,
    mem_recv,
    all_recv,
    load_sem,
    send_sem,
    recv_sem,
    met_sem,
):
    members, lats, lons = sizes
    zs = members // 2
    quads = 2 * lats
    share = -(-PRED_TILES // members)
    chunk = -(-PART // quads)
    me_m = lax.axis_index("member")
    me_a = lax.axis_index("lat")
    me_o = lax.axis_index("lon")
    me_z = me_m // 2
    me_h = me_m % 2
    me_q = me_h * lats + me_a

    loads = [
        pltpu.make_async_copy(src, dst, load_sem.at[i])
        for i, (src, dst) in enumerate(
            (
                (x_hbm.at[0], x16),
                (t_hbm, t16),
                (w_in_hbm, w_in_t),
                (w_out_hbm, w_out),
                (bias_ref, bias16),
            )
        )
    ]
    for load in loads:
        load.start()

    def at(dm_z, dm_h, da, do):
        return (
            ((me_z + dm_z) % zs) * 2 + (me_h + dm_h) % 2,
            (me_a + da + lats) % lats,
            (me_o + do + lons) % lons,
        )

    halo = [(da, do) for da, do in ((-1, -1), (-1, 1), (1, -1), (1, 1), (0, -1), (0, 1), (-1, 0), (1, 0))]
    group_m = [(dz, h) for dz in ring_order(zs) for h in (1, 0) if dz or h]
    group_q = [(h, da) for h in (1, 0) for da in ring_order(lats) if h or da]
    group_o = [d for d in ring_order(lons) if d]
    group_z = [d for d in ring_order(zs) if d]

    barrier = pltpu.get_barrier_semaphore()
    near = [at(0, 0, da, do) for da, do in halo] + [at(1, 0, 0, 0), at(zs - 1, 0, 0, 0), at(0, 1, 0, 0)]
    for device in near:
        pl.semaphore_signal(barrier, inc=1, device_id=device, device_id_type=MESH)

    steps = [at(1, 0, 0, 0), at(zs - 1, 0, 0, 0), at(0, 1, 0, 0)]
    steps += [at(0, 0, da, do) for da, do in halo if da == 0 or do == 0]

    def tell(wave):
        for device in steps:
            pl.semaphore_signal(met_sem.at[wave], inc=1, device_id=device, device_id_type=MESH)

    def hear(wave):
        pl.semaphore_wait(met_sem.at[wave], len(steps))

    loads[0].wait()
    loads[1].wait()
    rows32[0:LEV] = x16[...].astype(F32)
    rows32[LEV:] = t16[...].astype(F32)
    for r in range(ROWS):
        start = LEAD + PITCH * (r + HALO) + HALO
        xf[:, start : start + COLS] = rows32[:, r, :]

    def place(first, height, width):
        lane = lax.broadcasted_iota(jnp.int32, (height, width), 1).astype(F32) + float(first)
        row = jnp.floor((lane + 0.5) * (1.0 / PITCH))
        return row, lane - PITCH * row

    left_edge = jnp.zeros((2 * LEV, 128), F32)
    right_edge = jnp.zeros((2 * LEV, 128), F32)
    for t in range(4, 22):
        row, col = place(t * 128, 2 * LEV, 128)
        here = (row >= HALO) & (row < HALO + ROWS)
        tile = xf[:, LEAD + t * 128 : LEAD + t * 128 + 128]
        left_edge += jnp.where(here & (col >= HALO) & (col < 2 * HALO), tile, 0.0)
        right_edge += jnp.where(here & (col >= COLS) & (col < COLS + HALO), tile, 0.0)
    side_send[0] = right_edge.astype(BF16)
    side_send[1] = left_edge.astype(BF16)
    band_send[0] = xf[:, LEAD + 17 * 128 : LEAD + 22 * 128].astype(BF16)
    band_send[1] = xf[:, LEAD + 4 * 128 : LEAD + 9 * 128].astype(BF16)

    pl.semaphore_wait(barrier, len(near))

    def send(src, dst, phase, device):
        copy = pltpu.make_async_remote_copy(
            src_ref=src,
            dst_ref=dst,
            send_sem=send_sem.at[phase],
            recv_sem=recv_sem.at[phase],
            device_id=device,
            device_id_type=MESH,
        )
        copy.start()

    def wait_recv(ref, phase):
        pltpu.make_async_remote_copy(
            src_ref=ref,
            dst_ref=ref,
            send_sem=send_sem.at[phase],
            recv_sem=recv_sem.at[phase],
            device_id=(me_m, me_a, (me_o + 1) % lons),
            device_id_type=MESH,
        ).wait_recv()

    def wait_send(ref, phase):
        pltpu.make_async_remote_copy(
            src_ref=ref,
            dst_ref=ref,
            send_sem=send_sem.at[phase],
            recv_sem=recv_sem.at[phase],
            device_id=(me_m, me_a, (me_o + 1) % lons),
            device_id_type=MESH,
        ).wait_send()

    for da in (-1, 1, 0):
        send(side_send.at[0], side_recv.at[0, 1 - da], 0, at(0, 0, da, 1))
        send(side_send.at[1], side_recv.at[1, 1 - da], 0, at(0, 0, da, -1))
    send(band_send.at[0], band_recv.at[0], 1, at(0, 0, 1, 0))
    send(band_send.at[1], band_recv.at[1], 1, at(0, 0, -1, 0))

    tell(0)

    for load in loads[2:]:
        load.wait()
    w_in[...] = w_in_t[...].astype(F32).T.astype(BF16)
    w_out_t[...] = w_out[...].astype(F32).T.astype(BF16)
    bias[...] = jnp.broadcast_to(bias16[...], (C, C)).T
    hear(0)
    tell(1)
    taps[:, 0:128] = jnp.zeros((TAPS, 128), F32)
    taps[:, FLAT - 128 : FLAT] = jnp.zeros((TAPS, 128), F32)
    xf[:, 0:LEAD] = jnp.zeros((2 * LEV, LEAD), F32)
    xf[:, LEAD + FLAT :] = jnp.zeros((2 * LEV, 128), F32)
    gp[:, 0 : PRED_FIRST * 128] = jnp.zeros((LEV, PRED_FIRST * 128), F32)
    gp[:, (PRED_FIRST + PRED_TILES) * 128 :] = jnp.zeros((LEV, PRED_FIRST * 128), F32)
    spare = members * share - PRED_TILES
    for u in range(PRED_TILES, PRED_TILES + spare):
        target_tiles[u] = jnp.zeros((LEV, 128), F32)
        pred_send[u % members, u // members] = jnp.zeros((LEV, 128), BF16)
    for p in range(2):
        part_sum[p, PART:] = jnp.zeros((quads * chunk - PART, 8, C), F32)
    row_low = jnp.where(me_a == 0, HALO, 0).astype(F32)
    row_high = jnp.where(me_a == lats - 1, HALO + ROWS, ROWS + 2 * HALO).astype(F32)
    row, col = place(0, 8, FLAT)
    masks[0] = jnp.where((row >= row_low) & (row < row_high), 1.0, 0.0)
    masks[1] = jnp.where(
        (row >= HALO) & (row < HALO + ROWS) & (col >= HALO) & (col < HALO + COLS), 1.0, 0.0
    )

    hear(1)
    tell(2)
    wait_recv(side_recv, 0)
    wait_recv(band_recv, 1)

    sides = [[side_recv[i, j].astype(F32) for j in range(3)] for i in range(2)]
    for t in range(26):
        row, col = place(t * 128, 2 * LEV, 128)
        tile = xf[:, LEAD + t * 128 : LEAD + t * 128 + 128]
        left, right = sides[0][1], sides[1][1]
        if t < 5:
            above = row < HALO
            tile = jnp.where(above, band_recv[0, :, t * 128 : t * 128 + 128].astype(F32), tile)
            left = jnp.where(above, sides[0][0], left)
            right = jnp.where(above, sides[1][0], right)
        if t >= 21:
            below = row >= HALO + ROWS
            tile = jnp.where(below, band_recv[1, :, (t - 21) * 128 : (t - 20) * 128].astype(F32), tile)
            left = jnp.where(below, sides[0][2], left)
            right = jnp.where(below, sides[1][2], right)
        tile = jnp.where(col < HALO, left, tile)
        tile = jnp.where(col >= HALO + COLS, right, tile)
        if t < 5 or t >= 21:
            tile = jnp.where((row >= row_low) & (row < row_high), tile, 0.0)
        xf[:, LEAD + t * 128 : LEAD + t * 128 + 128] = tile
        if PRED_FIRST <= t < PRED_FIRST + PRED_TILES:
            target_tiles[t - PRED_FIRST] = tile[LEV:]

    hear(2)
    tell(3)

    for k, shift in enumerate(SHIFTS):
        xc[k * LEV : (k + 1) * LEV, 128:3200] = xf[0:LEV, LEAD + 128 + shift : LEAD + 3200 + shift].astype(BF16)

    def mask(which, first, last):
        return masks[which, 0:1, first:last] > 0.5

    hidden = jnp.dot(w_in[...], xc[:, 128:3200], preferred_element_type=F32)
    hidden += jnp.concatenate([bias[...]] * 24, axis=1)
    pre[:, 128:3200] = hidden
    value = jnp.where(mask(0, 128, 3200), hidden * jax.nn.sigmoid(hidden), 0.0).astype(BF16)
    act[:, 128:3200] = value
    taps[:, 128:3200] = jnp.dot(w_out[...], value, preferred_element_type=F32)

    for t in range(0, PRED_TILES, 2):
        first = (PRED_FIRST + t) * 128
        total = xf[0:LEV, LEAD + first : LEAD + first + 256]
        for k, shift in enumerate(SHIFTS):
            total += taps[k * LEV : (k + 1) * LEV, first + shift : first + shift + 256]
        for u in (t, t + 1):
            pred_send[u % members, u // members] = total[:, (u - t) * 128 : (u - t + 1) * 128].astype(BF16)

    hear(3)
    for dz, h in group_m:
        device = at(dz, h, 0, 0)
        send(pred_send.at[device[0]], pred_recv.at[me_m], 2, device)
    pred_recv[me_m] = pred_send[me_m]

    hidden = pre[:, 384:2944]
    gate = jax.nn.sigmoid(hidden)
    pre[:, 384:2944] = gate * (1.0 + hidden * (1.0 - gate))
    act_own[:, 384:2944] = jnp.where(
        mask(1, 384, 2944), act[:, 384:2944].astype(F32), 0.0
    ).astype(BF16)
    wait_recv(pred_recv.at[pl.ds(0, members - 1)], 2)

    coupling = (1.0 - 0.05 / members) / (members - 1)

    def slope(d):
        return d * lax.rsqrt(d * d + 0.25)

    for u in range(share):
        everyone = pred_recv[:, u].astype(F32)
        wanted = target_tiles[me_m + u * members]
        for half in range(2):
            own = everyone[:, half * 8 : half * 8 + 8]
            spread = jnp.zeros_like(own)
            for d in range(1, members // 2 + 1):
                term = slope(own - jnp.concatenate([own[d:], own[:d]], axis=0))
                spread += term
                if 2 * d != members:
                    spread -= jnp.concatenate([term[members - d :], term[: members - d]], axis=0)
            value = slope(own - wanted[None, half * 8 : half * 8 + 8]) - coupling * spread
            grads[:, half * 8 : half * 8 + 8, :] = value
        grad_send[:, u] = grads[...].astype(BF16)

    for dz, h in group_m:
        device = at(dz, h, 0, 0)
        send(grad_send.at[device[0]], grad_recv.at[me_m], 3, device)
    grad_recv[me_m] = grad_send[me_m]
    wait_recv(grad_recv.at[pl.ds(0, members - 1)], 3)

    for u in range(PRED_TILES):
        t = PRED_FIRST + u
        row, col = place(t * 128, LEV, 128)
        inside = (row >= row_low) & (row < row_high) & (col >= HALO - 2) & (col < HALO + COLS + 2)
        tile = grad_recv[u % members, u // members].astype(F32)
        gp[:, t * 128 : t * 128 + 128] = jnp.where(inside, tile, 0.0)
    for k, shift in enumerate(SHIFTS):
        gc[k * LEV : (k + 1) * LEV, 384:2944] = gp[:, 384 - shift : 2944 - shift].astype(BF16)

    contract_lanes = (((1,), (1,)), ((), ()))
    out_part = lax.dot_general(
        gc[:, 512:2816], act_own[:, 512:2816], contract_lanes, preferred_element_type=F32
    )
    part_sum[0, 0:PART] = out_part.reshape(PART, 8, C)
    for h, da in group_q:
        device = at(0, h, da, 0)
        slot = (device[0] % 2) * lats + device[1]
        send(part_sum.at[0, pl.ds(slot * chunk, chunk)], part_recv.at[0, me_q], 4, device)

    value = jnp.dot(w_out_t[...], gc[:, 384:2944], preferred_element_type=F32) * pre[:, 384:2944]
    gh_own[:, 384:2944] = jnp.where(mask(1, 384, 2944), value, 0.0).astype(BF16)
    gh[:, 384:2944] = jnp.where(mask(0, 384, 2944), value, 0.0).astype(BF16)
    in_part = lax.dot_general(
        xc[:, 512:2816], gh_own[:, 512:2816], contract_lanes, preferred_element_type=F32
    )
    part_sum[1, 0:PART] = in_part.reshape(PART, 8, C)
    for h, da in group_q:
        device = at(0, h, da, 0)
        slot = (device[0] % 2) * lats + device[1]
        send(part_sum.at[1, pl.ds(slot * chunk, chunk)], part_recv.at[1, me_q], 5, device)
    for p in range(2):
        part_recv[p, me_q] = part_sum[p, pl.ds(me_q * chunk, chunk)]

    def total_of(ref, count):
        total = ref[0]
        for i in range(1, count):
            total += ref[i]
        return total

    def to_lons(p, phase):
        for d in group_o:
            send(lon_recv.at[p, me_o], lon_recv.at[p, me_o], phase, at(0, 0, 0, d))

    def to_zs(p, phase):
        for d in group_z:
            send(mem_recv.at[p, me_z], mem_recv.at[p, me_z], phase, at(d, 0, 0, 0))

    wait_recv(part_recv.at[0, pl.ds(0, quads - 1)], 4)
    lon_recv[0, me_o] = total_of(part_recv.at[0], quads)
    to_lons(0, 6)

    taps[:, 384:2944] = jnp.dot(w_in_t[...], gh[:, 384:2944], preferred_element_type=F32)
    for r in range(ROWS):
        start = PITCH * (r + HALO) + HALO
        total = gp[:, start : start + COLS]
        for k, shift in enumerate(SHIFTS):
            total += taps[k * LEV : (k + 1) * LEV, start - shift : start - shift + COLS]
        by_row[r] = total
    for level in range(LEV):
        field[level] = by_row[:, level, :]

    wait_recv(part_recv.at[1, pl.ds(0, quads - 1)], 5)
    mem_recv[1, me_z] = total_of(part_recv.at[1], quads)
    to_zs(1, 7)
    wait_recv(lon_recv.at[0, pl.ds(0, lons - 1)], 6)
    mem_recv[0, me_z] = total_of(lon_recv.at[0], lons)
    to_zs(0, 8)
    wait_recv(mem_recv.at[1, pl.ds(0, zs - 1)], 7)
    lon_recv[1, me_o] = total_of(mem_recv.at[1], zs)
    to_lons(1, 9)
    scale = 1.0 / math.sqrt(members * lats * lons * ROWS * COLS)
    wait_recv(mem_recv.at[0, pl.ds(0, zs - 1)], 8)
    all_recv[0, me_q] = total_of(mem_recv.at[0], zs) * scale
    for h, da in group_q:
        send(all_recv.at[0, me_q], all_recv.at[0, me_q], 10, at(0, h, da, 0))
    wait_recv(lon_recv.at[1, pl.ds(0, lons - 1)], 9)
    all_recv[1, me_q] = total_of(lon_recv.at[1], lons) * scale
    for h, da in group_q:
        send(all_recv.at[1, me_q], all_recv.at[1, me_q], 11, at(0, h, da, 0))

    wait_send(side_recv, 0)
    wait_send(band_recv, 1)
    wait_send(pred_recv.at[pl.ds(0, members - 1)], 2)
    wait_send(grad_recv.at[pl.ds(0, members - 1)], 3)
    for p in range(2):
        wait_send(part_recv.at[p, pl.ds(0, quads - 1)], 4 + p)
        wait_send(lon_recv.at[p, pl.ds(0, lons - 1)], 6 + 3 * p)
        wait_send(mem_recv.at[p, pl.ds(0, zs - 1)], 8 - p)
    for p in range(2):
        wait_recv(all_recv.at[p, pl.ds(0, quads - 1)], 10 + p)
        for t in range(PART):
            sums_ref[p, t] = all_recv[p, t // chunk, t % chunk]
    for p in range(2):
        wait_send(all_recv.at[p, pl.ds(0, quads - 1)], 10 + p)


def write_out(field, sums, field_out, gin_out, gout_out, sem):
    copies = [
        pltpu.make_async_copy(src, dst, sem.at[i])
        for i, (src, dst) in enumerate(
            ((field, field_out.at[0]), (sums.at[1], gin_out), (sums.at[0], gout_out))
        )
    ]
    for copy in copies:
        copy.start()
    for copy in copies:
        copy.wait()


def shards(sizes, inputs, target, conv_in, bias_in, conv_out):
    members, lats, lons = sizes
    quads = 2 * lats
    share = -(-PRED_TILES // members)
    chunk = -(-PART // quads)
    wide = FLAT + LEAD + 128
    anywhere = pl.BlockSpec(memory_space=pl.ANY)
    near = pl.BlockSpec(memory_space=pltpu.VMEM)
    field, sums = pl.pallas_call(
        functools.partial(kernel, sizes),
        out_shape=(
            pltpu.VMEM((LEV, ROWS, COLS), F32),
            pltpu.VMEM((2, PART, 8, C), F32),
        ),
        in_specs=[pl.BlockSpec(memory_space=pltpu.HBM)] * 5,
        out_specs=(near, near),
        scratch_shapes=[
            pltpu.VMEM((LEV, ROWS, COLS), BF16),
            pltpu.VMEM((LEV, ROWS, COLS), BF16),
            pltpu.VMEM((TAPS, C), BF16),
            pltpu.VMEM((TAPS, C), BF16),
            pltpu.VMEM((1, C), F32),
            pltpu.VMEM((2 * LEV, ROWS, COLS), F32),
            pltpu.VMEM((2 * LEV, wide), F32),
            pltpu.VMEM((C, TAPS), BF16),
            pltpu.VMEM((C, TAPS), BF16),
            pltpu.VMEM((C, C), F32),
            pltpu.VMEM((2, 8, FLAT), F32),
            pltpu.VMEM((2, 2 * LEV, 128), BF16),
            pltpu.VMEM((2, 2 * LEV, 640), BF16),
            pltpu.VMEM((2, 3, 2 * LEV, 128), BF16),
            pltpu.VMEM((2, 2 * LEV, 640), BF16),
            pltpu.VMEM((TAPS, FLAT), BF16),
            pltpu.VMEM((C, FLAT), F32),
            pltpu.VMEM((C, FLAT), BF16),
            pltpu.VMEM((C, FLAT), BF16),
            pltpu.VMEM((TAPS, FLAT), F32),
            pltpu.VMEM((members, share, LEV, 128), BF16),
            pltpu.VMEM((members, share, LEV, 128), BF16),
            pltpu.VMEM((members * share, LEV, 128), F32),
            pltpu.VMEM((members, LEV, 128), F32),
            pltpu.VMEM((members, share, LEV, 128), BF16),
            pltpu.VMEM((members, share, LEV, 128), BF16),
            pltpu.VMEM((LEV, FLAT), F32),
            pltpu.VMEM((TAPS, FLAT), BF16),
            pltpu.VMEM((C, FLAT), BF16),
            pltpu.VMEM((C, FLAT), BF16),
            pltpu.VMEM((ROWS, LEV, COLS), F32),
            pltpu.VMEM((2, quads * chunk, 8, C), F32),
            pltpu.VMEM((2, quads, chunk, 8, C), F32),
            pltpu.VMEM((2, lons, chunk, 8, C), F32),
            pltpu.VMEM((2, members // 2, chunk, 8, C), F32),
            pltpu.VMEM((2, quads, chunk, 8, C), F32),
            pltpu.SemaphoreType.DMA((5,)),
            pltpu.SemaphoreType.DMA((12,)),
            pltpu.SemaphoreType.DMA((12,)),
            pltpu.SemaphoreType.REGULAR((4,)),
        ],
        compiler_params=pltpu.CompilerParams(
            collective_id=0, has_side_effects=True, vmem_limit_bytes=VMEM_LIMIT
        ),
        name="downscaling_step",
    )(
        *(
            pltpu.with_memory_space_constraint(operand, pltpu.HBM)
            for operand in (
                inputs,
                target,
                conv_in.transpose(0, 2, 1).reshape(TAPS, C),
                bias_in.reshape(1, C),
                conv_out.reshape(TAPS, C),
            )
        )
    )
    field, gin, gout = pl.pallas_call(
        write_out,
        out_shape=(
            jax.ShapeDtypeStruct((1, LEV, ROWS, COLS), F32),
            jax.ShapeDtypeStruct((PART, 8, C), F32),
            jax.ShapeDtypeStruct((PART, 8, C), F32),
        ),
        in_specs=[near] * 2,
        out_specs=(anywhere,) * 3,
        scratch_shapes=[pltpu.SemaphoreType.DMA((3,))],
        compiler_params=pltpu.CompilerParams(vmem_limit_bytes=1024 * 1024),
        name="write_out",
    )(field, sums)
    return field, gin.reshape(9, LEV, C).transpose(0, 2, 1), gout.reshape(9, LEV, C)


def solution(mesh):
    sizes = tuple(mesh.shape[axis] for axis in ("member", "lat", "lon"))
    in_specs = (P("member", None, "lat", "lon"), P(None, "lat", "lon"), P(), P(), P())
    out_specs = (P("member", None, "lat", "lon"), P(), P())
    return jax.shard_map(
        functools.partial(shards, sizes),
        mesh=mesh,
        in_specs=in_specs,
        out_specs=out_specs,
        check_vma=False,
    )
```

```python
import functools
import math

import jax
import jax.numpy as jnp
from jax import lax
from jax.experimental import pallas as pl
from jax.experimental.pallas import tpu as pltpu
from jax.sharding import PartitionSpec as P

MESH = pl.DeviceIdType.MESH
F32 = jnp.float32
BF16 = jnp.bfloat16
SUM = jnp.bfloat16

LEV = 16
C = 128
ROWS = 16
COLS = 128
HALO = 4
PITCH = COLS + 2 * HALO
FLAT = 26 * 128
LEAD = 128
OFFSETS = [(di, dj) for di in (-1, 0, 1) for dj in (-1, 0, 1)]
SHIFTS = [di * PITCH + dj for di, dj in OFFSETS]
PRED_FIRST = 2
PRED_TILES = 22
TAPS = 9 * LEV
VMEM_LIMIT = 40 * 1024 * 1024


def ring_order(count):
    return sorted(range(count), key=lambda d: (-min(d, count - d), d))


def shares(members):
    share = max(2, -(-PRED_TILES // members))
    return share, -(-PRED_TILES // share)


def kernel(
    sizes,
    x_hbm,
    t_hbm,
    w_in_hbm,
    bias_ref,
    w_out_hbm,
    field,
    sums_ref,
    x16,
    t16,
    w_in_t,
    w_out,
    bias16,
    rows32,
    xf,
    w_in,
    w_out_t,
    bias,
    masks,
    side_send,
    band_send,
    side_recv,
    band_recv,
    xc,
    pre,
    act,
    act_own,
    taps,
    pred_send,
    pred_recv,
    target_tiles,
    grads,
    grad_send,
    grad_recv,
    gp,
    gc,
    gh,
    gh_own,
    by_row,
    part_sum,
    part_recv,
    spare_recv,
    lon_recv,
    mem_recv,
    all_recv,
    load_sem,
    send_sem,
    recv_sem,
    met_sem,
):
    members, lats, lons = sizes
    zs = members // 2
    quads = 2 * lats
    share, owners = shares(members)
    me_m = lax.axis_index("member")
    me_a = lax.axis_index("lat")
    me_o = lax.axis_index("lon")
    me_z = me_m // 2
    me_h = me_m % 2
    me_q = me_h * lats + me_a

    loads = [
        pltpu.make_async_copy(src, dst, load_sem.at[i])
        for i, (src, dst) in enumerate(
            (
                (x_hbm.at[0], x16),
                (t_hbm, t16),
                (w_in_hbm, w_in_t),
                (w_out_hbm, w_out),
                (bias_ref, bias16),
            )
        )
    ]
    for load in loads:
        load.start()

    def at(dm_z, dm_h, da, do):
        return (
            ((me_z + dm_z) % zs) * 2 + (me_h + dm_h) % 2,
            (me_a + da + lats) % lats,
            (me_o + do + lons) % lons,
        )

    halo = [(da, do) for da, do in ((-1, -1), (-1, 1), (1, -1), (1, 1), (0, -1), (0, 1), (-1, 0), (1, 0))]
    group_m = [(dz, h) for dz in ring_order(zs) for h in (1, 0) if dz or h]
    group_q = [(1, 0), (1, 1), (1, 3), (1, 2), (0, 2), (0, 1), (0, 3)]
    group_o = [d for d in ring_order(lons) if d]
    group_z = [d for d in ring_order(zs) if d]

    barrier = pltpu.get_barrier_semaphore()
    near = [at(0, 0, da, do) for da, do in halo] + [at(0, 1, 0, 0)]
    near += [at(dz, 0, 0, 0) for dz in (1, zs - 1, 2, zs - 2)] + [at(0, 0, 0, do) for do in (2, -2)]
    for device in near:
        pl.semaphore_signal(barrier, inc=1, device_id=device, device_id_type=MESH)

    steps = [at(dz, 0, 0, 0) for dz in (2, zs - 2, 1, zs - 1)] + [at(0, 0, 0, do) for do in (2, -2)]
    steps += [at(0, 0, da, 0) for da in (1, -1)]

    def tell(wave):
        for device in steps:
            pl.semaphore_signal(met_sem.at[wave], inc=1, device_id=device, device_id_type=MESH)

    def hear(wave):
        pl.semaphore_wait(met_sem.at[wave], len(steps))

    loads[0].wait()
    loads[1].wait()
    rows32[0:LEV] = x16[...].astype(F32)
    rows32[LEV:] = t16[...].astype(F32)
    for r in range(ROWS):
        start = LEAD + PITCH * (r + HALO) + HALO
        xf[:, start : start + COLS] = rows32[:, r, :]

    def place(first, height, width):
        lane = lax.broadcasted_iota(jnp.int32, (height, width), 1).astype(F32) + float(first)
        row = jnp.floor((lane + 0.5) * (1.0 / PITCH))
        return row, lane - PITCH * row

    for part in range(2):
        chans = slice(part * LEV, (part + 1) * LEV)
        left_edge = jnp.zeros((LEV, 128), F32)
        right_edge = jnp.zeros((LEV, 128), F32)
        for t in range(4, 22):
            row, col = place(t * 128, LEV, 128)
            here = (row >= HALO) & (row < HALO + ROWS)
            tile = xf[chans, LEAD + t * 128 : LEAD + t * 128 + 128]
            left_edge += jnp.where(here & (col >= HALO) & (col < 2 * HALO), tile, 0.0)
            right_edge += jnp.where(here & (col >= COLS) & (col < COLS + HALO), tile, 0.0)
        side_send[part, 0] = right_edge.astype(BF16)
        side_send[part, 1] = left_edge.astype(BF16)
        band_send[part, 0] = xf[chans, LEAD + 17 * 128 : LEAD + 22 * 128].astype(BF16)
        band_send[part, 1] = xf[chans, LEAD + 4 * 128 : LEAD + 9 * 128].astype(BF16)

    pl.semaphore_wait(barrier, len(near))

    def send(src, dst, phase, device):
        copy = pltpu.make_async_remote_copy(
            src_ref=src,
            dst_ref=dst,
            send_sem=send_sem.at[phase],
            recv_sem=recv_sem.at[phase],
            device_id=device,
            device_id_type=MESH,
        )
        copy.start()

    def wait_recv(ref, phase):
        pltpu.make_async_remote_copy(
            src_ref=ref,
            dst_ref=ref,
            send_sem=send_sem.at[phase],
            recv_sem=recv_sem.at[phase],
            device_id=(me_m, me_a, (me_o + 1) % lons),
            device_id_type=MESH,
        ).wait_recv()

    def wait_send(ref, phase):
        pltpu.make_async_remote_copy(
            src_ref=ref,
            dst_ref=ref,
            send_sem=send_sem.at[phase],
            recv_sem=recv_sem.at[phase],
            device_id=(me_m, me_a, (me_o + 1) % lons),
            device_id_type=MESH,
        ).wait_send()

    for part in range(2):
        for da in (-1, 1, 0):
            send(side_send.at[part, 0], side_recv.at[part, 0, 1 - da], 2 * part, at(0, 0, da, 1))
            send(side_send.at[part, 1], side_recv.at[part, 1, 1 - da], 2 * part, at(0, 0, da, -1))
        send(band_send.at[part, 0], band_recv.at[part, 0], 2 * part + 1, at(0, 0, 1, 0))
        send(band_send.at[part, 1], band_recv.at[part, 1], 2 * part + 1, at(0, 0, -1, 0))
    tell(0)

    for load in loads[2:]:
        load.wait()
    w_in[...] = w_in_t[...].astype(F32).T.astype(BF16)
    w_out_t[...] = w_out[...].astype(F32).T.astype(BF16)
    bias[...] = jnp.broadcast_to(bias16[...], (C, C)).T
    taps[:, 0:128] = jnp.zeros((TAPS, 128), F32)
    taps[:, FLAT - 128 : FLAT] = jnp.zeros((TAPS, 128), F32)
    xf[:, 0:LEAD] = jnp.zeros((2 * LEV, LEAD), F32)
    xf[:, LEAD + FLAT :] = jnp.zeros((2 * LEV, 128), F32)
    gp[:, 0 : PRED_FIRST * 128] = jnp.zeros((LEV, PRED_FIRST * 128), F32)
    gp[:, (PRED_FIRST + PRED_TILES) * 128 :] = jnp.zeros((LEV, PRED_FIRST * 128), F32)
    for u in range(PRED_TILES, owners * share):
        target_tiles[u] = jnp.zeros((LEV, 128), F32)
        pred_send[u % owners, u // owners] = jnp.zeros((LEV, 128), BF16)
    lon_recv[me_o, 2] = jnp.zeros((LEV, C), SUM)
    row_low = jnp.where(me_a == 0, HALO, 0).astype(F32)
    row_high = jnp.where(me_a == lats - 1, HALO + ROWS, ROWS + 2 * HALO).astype(F32)
    row, col = place(0, 8, FLAT)
    masks[0] = jnp.where((row >= row_low) & (row < row_high), 1.0, 0.0)
    masks[1] = jnp.where(
        (row >= HALO) & (row < HALO + ROWS) & (col >= HALO) & (col < HALO + COLS), 1.0, 0.0
    )

    hear(0)
    tell(1)
    wait_recv(side_recv.at[0], 0)
    wait_recv(band_recv.at[0], 1)

    def unpack(part):
        chans = slice(part * LEV, (part + 1) * LEV)
        sides = [[side_recv[part, i, j].astype(F32) for j in range(3)] for i in range(2)]
        for t in range(26):
            row, col = place(t * 128, LEV, 128)
            lanes = slice(LEAD + t * 128, LEAD + t * 128 + 128)
            tile = xf[chans, lanes]
            left, right = sides[0][1], sides[1][1]
            if t < 5:
                above = row < HALO
                band = band_recv[part, 0, :, t * 128 : t * 128 + 128].astype(F32)
                tile = jnp.where(above, band, tile)
                left = jnp.where(above, sides[0][0], left)
                right = jnp.where(above, sides[1][0], right)
            if t >= 21:
                below = row >= HALO + ROWS
                band = band_recv[part, 1, :, (t - 21) * 128 : (t - 20) * 128].astype(F32)
                tile = jnp.where(below, band, tile)
                left = jnp.where(below, sides[0][2], left)
                right = jnp.where(below, sides[1][2], right)
            tile = jnp.where(col < HALO, left, tile)
            tile = jnp.where(col >= HALO + COLS, right, tile)
            if t < 5 or t >= 21:
                tile = jnp.where((row >= row_low) & (row < row_high), tile, 0.0)
            if part == 0:
                xf[chans, lanes] = tile
            elif PRED_FIRST <= t < PRED_FIRST + PRED_TILES:
                target_tiles[t - PRED_FIRST] = tile

    unpack(0)
    for k, shift in enumerate(SHIFTS):
        xc[k * LEV : (k + 1) * LEV, 128:3200] = xf[0:LEV, LEAD + 128 + shift : LEAD + 3200 + shift].astype(BF16)

    def mask(which, first, last):
        return masks[which, 0:1, first:last] > 0.5

    hidden = jnp.dot(w_in[...], xc[:, 128:3200], preferred_element_type=F32)
    hidden += jnp.concatenate([bias[...]] * 24, axis=1)
    pre[:, 128:3200] = hidden
    value = jnp.where(mask(0, 128, 3200), hidden * jax.nn.sigmoid(hidden), 0.0).astype(BF16)
    act[:, 128:3200] = value
    taps[:, 128:3200] = jnp.dot(w_out[...], value, preferred_element_type=F32)

    for t in range(0, PRED_TILES, 11):
        first, width = (PRED_FIRST + t) * 128, 11 * 128
        total = xf[0:LEV, LEAD + first : LEAD + first + width]
        for k, shift in enumerate(SHIFTS):
            total += taps[k * LEV : (k + 1) * LEV, first + shift : first + shift + width]
        for u in range(11):
            pred_send[(t + u) % owners, (t + u) // owners] = total[:, u * 128 : (u + 1) * 128].astype(BF16)

    hear(1)
    def rank(z, h):
        return ((z - zs + 3 + zs) % zs) * 2 + h

    me_r = rank(me_z, me_h)
    for dz, h in group_m:
        device = at(dz, h, 0, 0)
        slot = rank(device[0] // 2, device[0] % 2)

        @pl.when(slot < owners)
        def _(device=device, slot=slot):
            send(pred_send.at[slot], pred_recv.at[me_m], 4, device)

    hidden = pre[:, 384:2944]
    gate = jax.nn.sigmoid(hidden)
    pre[:, 384:2944] = gate * (1.0 + hidden * (1.0 - gate))
    act_own[:, 384:2944] = jnp.where(
        mask(1, 384, 2944), act[:, 384:2944].astype(F32), 0.0
    ).astype(BF16)
    wait_recv(side_recv.at[1], 2)
    wait_recv(band_recv.at[1], 3)
    unpack(1)

    coupling = (1.0 - 0.05 / members) / (members - 1)

    def slope(d):
        return d * lax.rsqrt(d * d + 0.25)

    @pl.when(me_r < owners)
    def _():
        pred_recv[me_m] = pred_send[me_r]
        wait_recv(pred_recv.at[pl.ds(0, members - 1)], 4)
        for u in range(share):
            everyone = pred_recv[:, u].astype(F32)
            wanted = target_tiles[me_r + u * owners]
            for half in range(2):
                own = everyone[:, half * 8 : half * 8 + 8]
                spread = jnp.zeros_like(own)
                for d in range(1, members // 2 + 1):
                    term = slope(own - jnp.concatenate([own[d:], own[:d]], axis=0))
                    spread += term
                    if 2 * d != members:
                        spread -= jnp.concatenate([term[members - d :], term[: members - d]], axis=0)
                value = slope(own - wanted[None, half * 8 : half * 8 + 8]) - coupling * spread
                grads[:, half * 8 : half * 8 + 8, :] = value
            grad_send[:, u] = grads[...].astype(BF16)
        for dz, h in group_m:
            device = at(dz, h, 0, 0)
            send(grad_send.at[device[0]], grad_recv.at[me_r], 5, device)
        grad_recv[me_r] = grad_send[me_m]
        wait_recv(grad_recv.at[pl.ds(0, owners - 1)], 5)

    @pl.when(me_r >= owners)
    def _():
        wait_recv(grad_recv, 5)

    for u in range(PRED_TILES):
        t = PRED_FIRST + u
        row, col = place(t * 128, LEV, 128)
        inside = (row >= row_low) & (row < row_high) & (col >= HALO - 2) & (col < HALO + COLS + 2)
        tile = grad_recv[u % owners, u // owners].astype(F32)
        gp[:, t * 128 : t * 128 + 128] = jnp.where(inside, tile, 0.0)
    for k, shift in enumerate(SHIFTS):
        gc[k * LEV : (k + 1) * LEV, 384:2944] = gp[:, 384 - shift : 2944 - shift].astype(BF16)

    spare_owner = (0, quads - 1)

    def in_group(q):
        return (me_z * 2 + q // lats, q % lats, me_o)

    def spread_part(p, value):
        part_sum[p] = value.reshape(9, LEV, C).astype(SUM)
        for h, da in group_q:
            device = at(0, h, da, 0)
            slot = (device[0] % 2) * lats + device[1]
            send(part_sum.at[p, slot], part_recv.at[p, me_q], 6 + p, device)

        @pl.when(me_q != spare_owner[p])
        def _():
            send(part_sum.at[p, 8], spare_recv.at[me_q], 8 + p, in_group(spare_owner[p]))

        part_recv[p, me_q] = part_sum[p, me_q]

    def total_of(ref, count):
        total = ref[0].astype(F32)
        for i in range(1, count):
            total += ref[i].astype(F32)
        return total

    contract_lanes = (((1,), (1,)), ((), ()))
    out_part = lax.dot_general(
        gc[:, 512:2816], act_own[:, 512:2816], contract_lanes, preferred_element_type=F32
    )
    spread_part(0, out_part)

    value = jnp.dot(w_out_t[...], gc[:, 384:2944], preferred_element_type=F32) * pre[:, 384:2944]
    gh_own[:, 384:2944] = jnp.where(mask(1, 384, 2944), value, 0.0).astype(BF16)
    gh[:, 384:2944] = jnp.where(mask(0, 384, 2944), value, 0.0).astype(BF16)
    in_part = lax.dot_general(
        xc[:, 512:2816], gh_own[:, 512:2816], contract_lanes, preferred_element_type=F32
    )
    spread_part(1, in_part)

    taps[:, 384:2944] = jnp.dot(w_in_t[...], gh[:, 384:2944], preferred_element_type=F32)
    for r in range(ROWS):
        start = PITCH * (r + HALO) + HALO
        total = gp[:, start : start + COLS]
        for k, shift in enumerate(SHIFTS):
            total += taps[k * LEV : (k + 1) * LEV, start - shift : start - shift + COLS]
        by_row[r] = total

    for p in range(2):
        wait_recv(part_recv.at[p, pl.ds(0, quads - 1)], 6 + p)
        lon_recv[me_o, p] = total_of(part_recv.at[p], quads).astype(SUM)
        others = spare_recv.at[pl.ds(0, quads - 1)]

        @pl.when(me_q == spare_owner[p])
        def _():
            spare_recv[me_q] = part_sum[p, 8]
            wait_recv(others, 8 + p)
            lon_recv[me_o, 2] = total_of(spare_recv, quads).astype(SUM)

    for d in group_o:
        send(lon_recv.at[me_o], lon_recv.at[me_o], 10, at(0, 0, 0, d))
    for level in range(LEV):
        field[level] = by_row[:, level, :]
    wait_recv(lon_recv.at[pl.ds(0, lons - 1)], 10)
    mem_recv[me_z] = total_of(lon_recv, lons).astype(SUM)
    for d in group_z:
        send(mem_recv.at[me_z], mem_recv.at[me_z], 11, at(d, 0, 0, 0))
    scale = 1.0 / math.sqrt(members * lats * lons * ROWS * COLS)
    wait_recv(mem_recv.at[pl.ds(0, zs - 1)], 11)
    all_recv[me_q] = (total_of(mem_recv, zs) * scale).astype(SUM)
    for h, da in group_q:
        send(all_recv.at[me_q], all_recv.at[me_q], 12, at(0, h, da, 0))

    for part in range(2):
        wait_send(side_recv.at[part], 2 * part)
        wait_send(band_recv.at[part], 2 * part + 1)
    @pl.when(me_r < owners)
    def _():
        wait_send(pred_send.at[pl.ds(0, owners - 1)], 4)
        wait_send(grad_send.at[pl.ds(0, members - 1)], 5)

    @pl.when(me_r >= owners)
    def _():
        wait_send(pred_send, 4)

    for p in range(2):
        wait_send(part_recv.at[p, pl.ds(0, quads - 1)], 6 + p)

        @pl.when(me_q != spare_owner[p])
        def _():
            wait_send(spare_recv.at[0], 8 + p)

    wait_send(lon_recv.at[pl.ds(0, lons - 1)], 10)
    wait_send(mem_recv.at[pl.ds(0, zs - 1)], 11)
    wait_recv(all_recv.at[pl.ds(0, quads - 1)], 12)
    for p in range(2):
        for t in range(9):
            value = all_recv[t, p] if t < 8 else all_recv[spare_owner[p], 2]
            sums_ref[p, t] = value.astype(F32)
    wait_send(all_recv.at[pl.ds(0, quads - 1)], 12)


def write_out(field, sums, field_out, gin_out, gout_out, sem):
    copies = [
        pltpu.make_async_copy(src, dst, sem.at[i])
        for i, (src, dst) in enumerate(
            ((field, field_out.at[0]), (sums.at[1], gin_out), (sums.at[0], gout_out))
        )
    ]
    for copy in copies:
        copy.start()
    for copy in copies:
        copy.wait()


def shards(sizes, inputs, target, conv_in, bias_in, conv_out):
    members, lats, lons = sizes
    quads = 2 * lats
    share, owners = shares(members)
    wide = FLAT + LEAD + 128
    anywhere = pl.BlockSpec(memory_space=pl.ANY)
    near = pl.BlockSpec(memory_space=pltpu.VMEM)
    field, sums = pl.pallas_call(
        functools.partial(kernel, sizes),
        out_shape=(
            pltpu.VMEM((LEV, ROWS, COLS), F32),
            pltpu.VMEM((2, 9, LEV, C), F32),
        ),
        in_specs=[pl.BlockSpec(memory_space=pltpu.HBM)] * 5,
        out_specs=(near, near),
        scratch_shapes=[
            pltpu.VMEM((LEV, ROWS, COLS), BF16),
            pltpu.VMEM((LEV, ROWS, COLS), BF16),
            pltpu.VMEM((TAPS, C), BF16),
            pltpu.VMEM((TAPS, C), BF16),
            pltpu.VMEM((1, C), F32),
            pltpu.VMEM((2 * LEV, ROWS, COLS), F32),
            pltpu.VMEM((2 * LEV, wide), F32),
            pltpu.VMEM((C, TAPS), BF16),
            pltpu.VMEM((C, TAPS), BF16),
            pltpu.VMEM((C, C), F32),
            pltpu.VMEM((2, 8, FLAT), F32),
            pltpu.VMEM((2, 2, LEV, 128), BF16),
            pltpu.VMEM((2, 2, LEV, 640), BF16),
            pltpu.VMEM((2, 2, 3, LEV, 128), BF16),
            pltpu.VMEM((2, 2, LEV, 640), BF16),
            pltpu.VMEM((TAPS, FLAT), BF16),
            pltpu.VMEM((C, FLAT), F32),
            pltpu.VMEM((C, FLAT), BF16),
            pltpu.VMEM((C, FLAT), BF16),
            pltpu.VMEM((TAPS, FLAT), F32),
            pltpu.VMEM((owners, share, LEV, 128), BF16),
            pltpu.VMEM((members, share, LEV, 128), BF16),
            pltpu.VMEM((owners * share, LEV, 128), F32),
            pltpu.VMEM((members, LEV, 128), F32),
            pltpu.VMEM((members, share, LEV, 128), BF16),
            pltpu.VMEM((owners, share, LEV, 128), BF16),
            pltpu.VMEM((LEV, FLAT), F32),
            pltpu.VMEM((TAPS, FLAT), BF16),
            pltpu.VMEM((C, FLAT), BF16),
            pltpu.VMEM((C, FLAT), BF16),
            pltpu.VMEM((ROWS, LEV, COLS), F32),
            pltpu.VMEM((2, 9, LEV, C), SUM),
            pltpu.VMEM((2, quads, LEV, C), SUM),
            pltpu.VMEM((quads, LEV, C), SUM),
            pltpu.VMEM((lons, 3, LEV, C), SUM),
            pltpu.VMEM((members // 2, 3, LEV, C), SUM),
            pltpu.VMEM((quads, 3, LEV, C), SUM),
            pltpu.SemaphoreType.DMA((5,)),
            pltpu.SemaphoreType.DMA((13,)),
            pltpu.SemaphoreType.DMA((13,)),
            pltpu.SemaphoreType.REGULAR((2,)),
        ],
        compiler_params=pltpu.CompilerParams(
            collective_id=0, has_side_effects=True, vmem_limit_bytes=VMEM_LIMIT
        ),
        name="downscaling_step",
    )(
        *(
            pltpu.with_memory_space_constraint(operand, pltpu.HBM)
            for operand in (
                inputs,
                target,
                conv_in.transpose(0, 2, 1).reshape(TAPS, C),
                bias_in.reshape(1, C),
                conv_out.reshape(TAPS, C),
            )
        )
    )
    field, gin, gout = pl.pallas_call(
        write_out,
        out_shape=(
            jax.ShapeDtypeStruct((1, LEV, ROWS, COLS), F32),
            jax.ShapeDtypeStruct((9, LEV, C), F32),
            jax.ShapeDtypeStruct((9, LEV, C), F32),
        ),
        in_specs=[near] * 2,
        out_specs=(anywhere,) * 3,
        scratch_shapes=[pltpu.SemaphoreType.DMA((3,))],
        compiler_params=pltpu.CompilerParams(vmem_limit_bytes=1024 * 1024),
        name="write_out",
    )(field, sums)
    return field, gin.transpose(0, 2, 1), gout


def solution(mesh):
    sizes = tuple(mesh.shape[axis] for axis in ("member", "lat", "lon"))
    in_specs = (P("member", None, "lat", "lon"), P(None, "lat", "lon"), P(), P(), P())
    out_specs = (P("member", None, "lat", "lon"), P(), P())
    return jax.shard_map(
        functools.partial(shards, sizes),
        mesh=mesh,
        in_specs=in_specs,
        out_specs=out_specs,
        check_vma=False,
    )
```

```python
import functools
import math

import jax
import jax.numpy as jnp
from jax import lax
from jax.experimental import pallas as pl
from jax.experimental.pallas import tpu as pltpu
from jax.sharding import PartitionSpec as P

MESH = pl.DeviceIdType.MESH
F32 = jnp.float32
BF16 = jnp.bfloat16
SUM = jnp.bfloat16

LEV = 16
C = 128
ROWS = 16
COLS = 128
HALO = 4
PITCH = COLS + 2 * HALO
FLAT = 26 * 128
LEAD = 128
OFFSETS = [(di, dj) for di in (-1, 0, 1) for dj in (-1, 0, 1)]
SHIFTS = [di * PITCH + dj for di, dj in OFFSETS]
PRED_FIRST = 2
PRED_TILES = 22
TAPS = 9 * LEV
VMEM_LIMIT = 40 * 1024 * 1024


def ring_order(count):
    return sorted(range(count), key=lambda d: (-min(d, count - d), d))


def shares(members):
    low, extra = divmod(PRED_TILES, members)
    return low, extra


def kernel(
    sizes,
    x_hbm,
    t_hbm,
    w_in_hbm,
    bias_ref,
    w_out_hbm,
    field,
    sums_ref,
    x16,
    t16,
    w_in_t,
    w_out,
    bias16,
    rows32,
    xf,
    w_in,
    w_out_t,
    bias,
    masks,
    side_send,
    band_send,
    side_recv,
    band_recv,
    xc,
    pre,
    act,
    act_t,
    xc_t,
    taps,
    pred_send,
    pred_recv,
    target_tiles,
    grads,
    grad_send,
    grad_recv,
    gp,
    gc,
    gh,
    gh_own,
    by_row,
    part_sum,
    part_recv,
    spare_recv,
    first,
    second,
    spare_first,
    spare_second,
    spare_all,
    all_recv,
    load_sem,
    send_sem,
    recv_sem,
    met_sem,
):
    members, lats, lons = sizes
    zs = members // 2
    quads = 2 * lats
    low, extra = shares(members)
    share = low + 1
    me_m = lax.axis_index("member")
    me_a = lax.axis_index("lat")
    me_o = lax.axis_index("lon")
    me_z = me_m // 2
    me_h = me_m % 2
    me_q = me_h * lats + me_a

    loads = [
        pltpu.make_async_copy(src, dst, load_sem.at[i])
        for i, (src, dst) in enumerate(
            (
                (x_hbm.at[0], x16),
                (t_hbm, t16),
                (w_in_hbm, w_in_t),
                (w_out_hbm, w_out),
                (bias_ref, bias16),
            )
        )
    ]
    for load in loads:
        load.start()

    def at(dm_z, dm_h, da, do):
        return (
            ((me_z + dm_z) % zs) * 2 + (me_h + dm_h) % 2,
            (me_a + da + lats) % lats,
            (me_o + do + lons) % lons,
        )

    halo = [(da, do) for da, do in ((-1, -1), (-1, 1), (1, -1), (1, 1), (0, -1), (0, 1), (-1, 0), (1, 0))]
    group_m = [(dz, h) for dz in ring_order(zs) for h in (1, 0) if dz or h]
    group_q = [(1, 0), (1, 1), (1, 3), (1, 2), (0, 2), (0, 1), (0, 3)]
    group_o = [d for d in ring_order(lons) if d]
    group_z = [d for d in ring_order(zs) if d]

    barrier = pltpu.get_barrier_semaphore()
    near = [at(0, 0, da, do) for da, do in halo] + [at(0, 1, 0, 0)]
    near += [at(dz, 0, 0, 0) for dz in (1, zs - 1, 2, zs - 2)] + [at(0, 0, 0, do) for do in (2, -2)]
    for device in near:
        pl.semaphore_signal(barrier, inc=1, device_id=device, device_id_type=MESH)

    steps = [at(dz, 0, 0, 0) for dz in (2, zs - 2, 1, zs - 1)] + [at(0, 0, 0, do) for do in (2, -2)]
    steps += [at(0, 0, da, 0) for da in (1, -1)]

    def tell(wave):
        for device in steps:
            pl.semaphore_signal(met_sem.at[wave], inc=1, device_id=device, device_id_type=MESH)

    def hear(wave):
        pl.semaphore_wait(met_sem.at[wave], len(steps))

    loads[0].wait()
    loads[1].wait()
    rows32[0:LEV] = x16[...].astype(F32)
    rows32[LEV:] = t16[...].astype(F32)
    for r in range(ROWS):
        start = LEAD + PITCH * (r + HALO) + HALO
        xf[:, start : start + COLS] = rows32[:, r, :]

    def place(first, height, width):
        lane = lax.broadcasted_iota(jnp.int32, (height, width), 1).astype(F32) + float(first)
        row = jnp.floor((lane + 0.5) * (1.0 / PITCH))
        return row, lane - PITCH * row

    for part in range(2):
        chans = slice(part * LEV, (part + 1) * LEV)
        left_edge = jnp.zeros((LEV, 128), F32)
        right_edge = jnp.zeros((LEV, 128), F32)
        for t in range(4, 22):
            row, col = place(t * 128, LEV, 128)
            here = (row >= HALO) & (row < HALO + ROWS)
            tile = xf[chans, LEAD + t * 128 : LEAD + t * 128 + 128]
            left_edge += jnp.where(here & (col >= HALO) & (col < 2 * HALO), tile, 0.0)
            right_edge += jnp.where(here & (col >= COLS) & (col < COLS + HALO), tile, 0.0)
        side_send[part, 0] = right_edge.astype(BF16)
        side_send[part, 1] = left_edge.astype(BF16)
        band_send[part, 0] = xf[chans, LEAD + 17 * 128 : LEAD + 22 * 128].astype(BF16)
        band_send[part, 1] = xf[chans, LEAD + 4 * 128 : LEAD + 9 * 128].astype(BF16)

    pl.semaphore_wait(barrier, len(near))

    def send(src, dst, phase, device):
        copy = pltpu.make_async_remote_copy(
            src_ref=src,
            dst_ref=dst,
            send_sem=send_sem.at[phase],
            recv_sem=recv_sem.at[phase],
            device_id=device,
            device_id_type=MESH,
        )
        copy.start()

    def wait_recv(ref, phase):
        pltpu.make_async_remote_copy(
            src_ref=ref,
            dst_ref=ref,
            send_sem=send_sem.at[phase],
            recv_sem=recv_sem.at[phase],
            device_id=(me_m, me_a, (me_o + 1) % lons),
            device_id_type=MESH,
        ).wait_recv()

    def wait_send(ref, phase):
        pltpu.make_async_remote_copy(
            src_ref=ref,
            dst_ref=ref,
            send_sem=send_sem.at[phase],
            recv_sem=recv_sem.at[phase],
            device_id=(me_m, me_a, (me_o + 1) % lons),
            device_id_type=MESH,
        ).wait_send()

    for part in range(2):
        for da in (-1, 1, 0):
            send(side_send.at[part, 0], side_recv.at[part, 0, 1 - da], 2 * part, at(0, 0, da, 1))
            send(side_send.at[part, 1], side_recv.at[part, 1, 1 - da], 2 * part, at(0, 0, da, -1))
        send(band_send.at[part, 0], band_recv.at[part, 0], 2 * part + 1, at(0, 0, 1, 0))
        send(band_send.at[part, 1], band_recv.at[part, 1], 2 * part + 1, at(0, 0, -1, 0))
    tell(0)

    for load in loads[2:]:
        load.wait()
    w_in[...] = w_in_t[...].astype(F32).T.astype(BF16)
    w_out_t[...] = w_out[...].astype(F32).T.astype(BF16)
    bias[...] = jnp.broadcast_to(bias16[...], (C, C)).T
    taps[:, 0:128] = jnp.zeros((TAPS, 128), F32)
    taps[:, FLAT - 128 : FLAT] = jnp.zeros((TAPS, 128), F32)
    xf[:, 0:LEAD] = jnp.zeros((2 * LEV, LEAD), F32)
    xf[:, LEAD + FLAT :] = jnp.zeros((2 * LEV, 128), F32)
    gp[:, 0 : PRED_FIRST * 128] = jnp.zeros((LEV, PRED_FIRST * 128), F32)
    gp[:, (PRED_FIRST + PRED_TILES) * 128 :] = jnp.zeros((LEV, PRED_FIRST * 128), F32)
    row_low = jnp.where(me_a == 0, HALO, 0).astype(F32)
    row_high = jnp.where(me_a == lats - 1, HALO + ROWS, ROWS + 2 * HALO).astype(F32)
    row, col = place(0, 8, FLAT)
    masks[0] = jnp.where((row >= row_low) & (row < row_high), 1.0, 0.0)
    masks[1] = jnp.where(
        (row >= HALO) & (row < HALO + ROWS) & (col >= HALO) & (col < HALO + COLS), 1.0, 0.0
    )

    hear(0)
    tell(1)
    wait_recv(side_recv.at[0], 0)
    wait_recv(band_recv.at[0], 1)

    def unpack(part):
        chans = slice(part * LEV, (part + 1) * LEV)
        sides = [[side_recv[part, i, j].astype(F32) for j in range(3)] for i in range(2)]
        for t in range(26):
            row, col = place(t * 128, LEV, 128)
            lanes = slice(LEAD + t * 128, LEAD + t * 128 + 128)
            tile = xf[chans, lanes]
            left, right = sides[0][1], sides[1][1]
            if t < 5:
                above = row < HALO
                band = band_recv[part, 0, :, t * 128 : t * 128 + 128].astype(F32)
                tile = jnp.where(above, band, tile)
                left = jnp.where(above, sides[0][0], left)
                right = jnp.where(above, sides[1][0], right)
            if t >= 21:
                below = row >= HALO + ROWS
                band = band_recv[part, 1, :, (t - 21) * 128 : (t - 20) * 128].astype(F32)
                tile = jnp.where(below, band, tile)
                left = jnp.where(below, sides[0][2], left)
                right = jnp.where(below, sides[1][2], right)
            tile = jnp.where(col < HALO, left, tile)
            tile = jnp.where(col >= HALO + COLS, right, tile)
            if t < 5 or t >= 21:
                tile = jnp.where((row >= row_low) & (row < row_high), tile, 0.0)
            if part == 0:
                xf[chans, lanes] = tile
            elif PRED_FIRST <= t < PRED_FIRST + PRED_TILES:
                target_tiles[t - PRED_FIRST] = tile

    unpack(0)
    for k, shift in enumerate(SHIFTS):
        xc[k * LEV : (k + 1) * LEV, 128:3200] = xf[0:LEV, LEAD + 128 + shift : LEAD + 3200 + shift].astype(BF16)

    def mask(which, first, last):
        return masks[which, 0:1, first:last] > 0.5

    hidden = jnp.dot(w_in[...], xc[:, 128:3200], preferred_element_type=F32)
    hidden += jnp.concatenate([bias[...]] * 24, axis=1)
    pre[:, 128:3200] = hidden
    value = jnp.where(mask(0, 128, 3200), hidden * jax.nn.sigmoid(hidden), 0.0).astype(BF16)
    act[:, 128:3200] = value
    taps[:, 128:3200] = jnp.dot(w_out[...], value, preferred_element_type=F32)

    for t in range(0, PRED_TILES, 11):
        begin, width = (PRED_FIRST + t) * 128, 11 * 128
        total = xf[0:LEV, LEAD + begin : LEAD + begin + width]
        for k, shift in enumerate(SHIFTS):
            total += taps[k * LEV : (k + 1) * LEV, begin + shift : begin + shift + width]
        for u in range(11):
            pred_send[t + u] = total[:, u * 128 : (u + 1) * 128].astype(BF16)

    hear(1)
    def rank(z, h):
        return ((z + 3) % zs) * 2 + h

    def tiles_of(ref, slot, more):
        start = slot * share if more else extra + slot * low
        return ref.at[pl.ds(start, share if more else low)]

    def either(slot, act_on):
        @pl.when(slot < extra)
        def _():
            act_on(True, share)

        @pl.when(slot >= extra)
        def _():
            act_on(False, low)

    me_r = rank(me_z, me_h)
    for dz, h in group_m:
        device = at(dz, h, 0, 0)
        slot = rank(device[0] // 2, device[0] % 2)

        def send_pred(more, count, device=device, slot=slot):
            dst = pred_recv.at[me_m, pl.ds(0, count)]
            send(tiles_of(pred_send, slot, more), dst, 4, device)

        either(slot, send_pred)

    hidden = pre[:, 384:2944]
    gate = jax.nn.sigmoid(hidden)
    pre[:, 384:2944] = gate * (1.0 + hidden * (1.0 - gate))
    act_t[...] = jnp.where(mask(1, 512, 2816), act[:, 512:2816].astype(F32), 0.0).T.astype(BF16)
    xc_t[...] = xc[:, 512:2816].astype(F32).T.astype(BF16)
    wait_recv(side_recv.at[1], 2)
    wait_recv(band_recv.at[1], 3)
    unpack(1)

    coupling = (1.0 - 0.05 / members) / (members - 1)

    def slope(d):
        return d * lax.rsqrt(d * d + 0.25)

    def own_tiles(more, count):
        start = me_r * share if more else extra + me_r * low
        for u in range(count):
            pred_recv[me_m, u] = pred_send[start + u]
        wait_recv(pred_recv.at[pl.ds(0, members - 1), pl.ds(0, count)], 4)
        for u in range(count):
            everyone = pred_recv[:, u].astype(F32)
            wanted = target_tiles[start + u]
            for half in range(2):
                own = everyone[:, half * 8 : half * 8 + 8]
                spread = jnp.zeros_like(own)
                for d in range(1, members // 2 + 1):
                    term = slope(own - jnp.concatenate([own[d:], own[:d]], axis=0))
                    spread += term
                    if 2 * d != members:
                        spread -= jnp.concatenate([term[members - d :], term[: members - d]], axis=0)
                value = slope(own - wanted[None, half * 8 : half * 8 + 8]) - coupling * spread
                grads[:, half * 8 : half * 8 + 8, :] = value
            grad_send[:, u] = grads[...].astype(BF16)
        for dz, h in group_m:
            device = at(dz, h, 0, 0)
            src = grad_send.at[device[0], pl.ds(0, count)]
            send(src, tiles_of(grad_recv, me_r, more), 5, device)
        for u in range(count):
            grad_recv[start + u] = grad_send[me_m, u]
        wait_recv(grad_recv.at[pl.ds(0, PRED_TILES - count)], 5)

    either(me_r, own_tiles)

    for u in range(PRED_TILES):
        t = PRED_FIRST + u
        row, col = place(t * 128, LEV, 128)
        inside = (row >= row_low) & (row < row_high) & (col >= HALO - 2) & (col < HALO + COLS + 2)
        tile = grad_recv[u].astype(F32)
        gp[:, t * 128 : t * 128 + 128] = jnp.where(inside, tile, 0.0)
    for k, shift in enumerate(SHIFTS):
        gc[k * LEV : (k + 1) * LEV, 384:2944] = gp[:, 384 - shift : 2944 - shift].astype(BF16)

    spare_owner = (0, quads - 1)

    def in_group(q):
        return (me_z * 2 + q // lats, q % lats, me_o)

    def spread_part(p, value):
        part_sum[p] = value.reshape(9, LEV, C).astype(SUM)
        for h, da in group_q:
            device = at(0, h, da, 0)
            slot = (device[0] % 2) * lats + device[1]
            send(part_sum.at[p, slot], part_recv.at[p, me_q], 6 + p, device)

        @pl.when(me_q != spare_owner[p])
        def _():
            send(part_sum.at[p, 8], spare_recv.at[me_q], 8 + p, in_group(spare_owner[p]))

        part_recv[p, me_q] = part_sum[p, me_q]

    def total_of(ref, count):
        total = ref[0].astype(F32)
        for i in range(1, count):
            total += ref[i].astype(F32)
        return total

    out_part = jnp.dot(gc[:, 512:2816], act_t[...], preferred_element_type=F32)
    spread_part(0, out_part)

    value = jnp.dot(w_out_t[...], gc[:, 384:2944], preferred_element_type=F32) * pre[:, 384:2944]
    gh_own[:, 384:2944] = jnp.where(mask(1, 384, 2944), value, 0.0).astype(BF16)
    gh[:, 384:2944] = jnp.where(mask(0, 384, 2944), value, 0.0).astype(BF16)
    in_part = jnp.dot(gh_own[:, 512:2816], xc_t[...], preferred_element_type=F32).T
    spread_part(1, in_part)

    taps[:, 384:2944] = jnp.dot(w_in_t[...], gh[:, 384:2944], preferred_element_type=F32)
    for r in range(ROWS):
        start = PITCH * (r + HALO) + HALO
        total = gp[:, start : start + COLS]
        for k, shift in enumerate(SHIFTS):
            total += taps[k * LEV : (k + 1) * LEV, start - shift : start - shift + COLS]
        by_row[r] = total

    by_lon = (me_o, lons, [at(0, 0, 0, d) for d in group_o])
    by_z = (me_z, zs, [at(d, 0, 0, 0) for d in group_z])
    first_axis, second_axis = (by_lon, by_z), (by_z, by_lon)

    def share_sum(value, dst, phase, axis):
        dst[axis[0]] = value.astype(SUM)
        for device in axis[2]:
            send(dst.at[axis[0]], dst.at[axis[0]], phase, device)

    for p in range(2):
        wait_recv(part_recv.at[p, pl.ds(0, quads - 1)], 6 + p)
        share_sum(total_of(part_recv.at[p], quads), first.at[p], 10 + p, first_axis[p])

        @pl.when(me_q == spare_owner[p])
        def _():
            spare_recv[me_q] = part_sum[p, 8]
            wait_recv(spare_recv.at[pl.ds(0, quads - 1)], 8 + p)
            share_sum(total_of(spare_recv, quads), spare_first, 14, first_axis[p])

    for level in range(LEV):
        field[level] = by_row[:, level, :]

    for p in range(2):
        count = first_axis[p][1]
        wait_recv(first.at[p, pl.ds(0, count - 1)], 10 + p)
        share_sum(total_of(first.at[p], count), second.at[p], 12 + p, second_axis[p])

        @pl.when(me_q == spare_owner[p])
        def _():
            wait_recv(spare_first.at[pl.ds(0, count - 1)], 14)
            share_sum(total_of(spare_first, count), spare_second, 15, second_axis[p])

    scale = 1.0 / math.sqrt(members * lats * lons * ROWS * COLS)
    for p in range(2):
        count = second_axis[p][1]
        wait_recv(second.at[p, pl.ds(0, count - 1)], 12 + p)
        all_recv[p, me_q] = (total_of(second.at[p], count) * scale).astype(SUM)
        for h, da in group_q:
            send(all_recv.at[p, me_q], all_recv.at[p, me_q], (16, 19)[p], at(0, h, da, 0))

        @pl.when(me_q == spare_owner[p])
        def _():
            wait_recv(spare_second.at[pl.ds(0, count - 1)], 15)
            spare_all[p] = (total_of(spare_second, count) * scale).astype(SUM)
            for h, da in group_q:
                send(spare_all.at[p], spare_all.at[p], 17 + p, at(0, h, da, 0))

    for part in range(2):
        wait_send(side_recv.at[part], 2 * part)
        wait_send(band_recv.at[part], 2 * part + 1)
    def all_sent(more, count):
        wait_send(pred_send.at[pl.ds(0, PRED_TILES - count)], 4)
        wait_send(grad_send.at[pl.ds(0, members - 1), pl.ds(0, count)], 5)

    either(me_r, all_sent)
    for p in range(2):
        wait_send(part_recv.at[p, pl.ds(0, quads - 1)], 6 + p)

        @pl.when(me_q != spare_owner[p])
        def _():
            wait_send(spare_recv.at[0], 8 + p)

    for p in range(2):
        wait_send(first.at[p, pl.ds(0, first_axis[p][1] - 1)], 10 + p)
        wait_send(second.at[p, pl.ds(0, second_axis[p][1] - 1)], 12 + p)

        @pl.when(me_q == spare_owner[p])
        def _():
            wait_send(spare_first.at[pl.ds(0, first_axis[p][1] - 1)], 14)
            wait_send(spare_second.at[pl.ds(0, second_axis[p][1] - 1)], 15)

    for p in range(2):
        wait_recv(all_recv.at[p, pl.ds(0, quads - 1)], (16, 19)[p])

        @pl.when(me_q != spare_owner[p])
        def _():
            wait_recv(spare_all.at[p], 17 + p)

        for t in range(8):
            sums_ref[p, t] = all_recv[p, t].astype(F32)
        sums_ref[p, 8] = spare_all[p].astype(F32)

    for p in range(2):
        wait_send(all_recv.at[p, pl.ds(0, quads - 1)], (16, 19)[p])

        @pl.when(me_q == spare_owner[p])
        def _():
            wait_send(spare_recv.at[pl.ds(0, quads - 1)], 17 + p)


def write_out(field, sums, field_out, gin_out, gout_out, sem):
    copies = [
        pltpu.make_async_copy(src, dst, sem.at[i])
        for i, (src, dst) in enumerate(
            ((field, field_out.at[0]), (sums.at[1], gin_out), (sums.at[0], gout_out))
        )
    ]
    for copy in copies:
        copy.start()
    for copy in copies:
        copy.wait()


def shards(sizes, inputs, target, conv_in, bias_in, conv_out):
    members, lats, lons = sizes
    quads = 2 * lats
    low, extra = shares(members)
    share = low + 1
    wide = FLAT + LEAD + 128
    anywhere = pl.BlockSpec(memory_space=pl.ANY)
    near = pl.BlockSpec(memory_space=pltpu.VMEM)
    field, sums = pl.pallas_call(
        functools.partial(kernel, sizes),
        out_shape=(
            pltpu.VMEM((LEV, ROWS, COLS), F32),
            pltpu.VMEM((2, 9, LEV, C), F32),
        ),
        in_specs=[pl.BlockSpec(memory_space=pltpu.HBM)] * 5,
        out_specs=(near, near),
        scratch_shapes=[
            pltpu.VMEM((LEV, ROWS, COLS), BF16),
            pltpu.VMEM((LEV, ROWS, COLS), BF16),
            pltpu.VMEM((TAPS, C), BF16),
            pltpu.VMEM((TAPS, C), BF16),
            pltpu.VMEM((1, C), F32),
            pltpu.VMEM((2 * LEV, ROWS, COLS), F32),
            pltpu.VMEM((2 * LEV, wide), F32),
            pltpu.VMEM((C, TAPS), BF16),
            pltpu.VMEM((C, TAPS), BF16),
            pltpu.VMEM((C, C), F32),
            pltpu.VMEM((2, 8, FLAT), F32),
            pltpu.VMEM((2, 2, LEV, 128), BF16),
            pltpu.VMEM((2, 2, LEV, 640), BF16),
            pltpu.VMEM((2, 2, 3, LEV, 128), BF16),
            pltpu.VMEM((2, 2, LEV, 640), BF16),
            pltpu.VMEM((TAPS, FLAT), BF16),
            pltpu.VMEM((C, FLAT), F32),
            pltpu.VMEM((C, FLAT), BF16),
            pltpu.VMEM((2304, C), BF16),
            pltpu.VMEM((2304, TAPS), BF16),
            pltpu.VMEM((TAPS, FLAT), F32),
            pltpu.VMEM((PRED_TILES, LEV, 128), BF16),
            pltpu.VMEM((members, share, LEV, 128), BF16),
            pltpu.VMEM((PRED_TILES, LEV, 128), F32),
            pltpu.VMEM((members, LEV, 128), F32),
            pltpu.VMEM((members, share, LEV, 128), BF16),
            pltpu.VMEM((PRED_TILES, LEV, 128), BF16),
            pltpu.VMEM((LEV, FLAT), F32),
            pltpu.VMEM((TAPS, FLAT), BF16),
            pltpu.VMEM((C, FLAT), BF16),
            pltpu.VMEM((C, FLAT), BF16),
            pltpu.VMEM((ROWS, LEV, COLS), F32),
            pltpu.VMEM((2, 9, LEV, C), SUM),
            pltpu.VMEM((2, quads, LEV, C), SUM),
            pltpu.VMEM((quads, LEV, C), SUM),
            pltpu.VMEM((2, max(lons, members // 2), LEV, C), SUM),
            pltpu.VMEM((2, max(lons, members // 2), LEV, C), SUM),
            pltpu.VMEM((max(lons, members // 2), LEV, C), SUM),
            pltpu.VMEM((max(lons, members // 2), LEV, C), SUM),
            pltpu.VMEM((2, LEV, C), SUM),
            pltpu.VMEM((2, quads, LEV, C), SUM),
            pltpu.SemaphoreType.DMA((5,)),
            pltpu.SemaphoreType.DMA((20,)),
            pltpu.SemaphoreType.DMA((20,)),
            pltpu.SemaphoreType.REGULAR((2,)),
        ],
        compiler_params=pltpu.CompilerParams(
            collective_id=0, has_side_effects=True, vmem_limit_bytes=VMEM_LIMIT
        ),
        name="downscaling_step",
    )(
        *(
            pltpu.with_memory_space_constraint(operand, pltpu.HBM)
            for operand in (
                inputs,
                target,
                conv_in.transpose(0, 2, 1).reshape(TAPS, C),
                bias_in.reshape(1, C),
                conv_out.reshape(TAPS, C),
            )
        )
    )
    field, gin, gout = pl.pallas_call(
        write_out,
        out_shape=(
            jax.ShapeDtypeStruct((1, LEV, ROWS, COLS), F32),
            jax.ShapeDtypeStruct((9, LEV, C), F32),
            jax.ShapeDtypeStruct((9, LEV, C), F32),
        ),
        in_specs=[near] * 2,
        out_specs=(anywhere,) * 3,
        scratch_shapes=[pltpu.SemaphoreType.DMA((3,))],
        compiler_params=pltpu.CompilerParams(vmem_limit_bytes=1024 * 1024),
        name="write_out",
    )(field, sums)
    return field, gin.transpose(0, 2, 1), gout


def solution(mesh):
    sizes = tuple(mesh.shape[axis] for axis in ("member", "lat", "lon"))
    in_specs = (P("member", None, "lat", "lon"), P(None, "lat", "lon"), P(), P(), P())
    out_specs = (P("member", None, "lat", "lon"), P(), P())
    return jax.shard_map(
        functools.partial(shards, sizes),
        mesh=mesh,
        in_specs=in_specs,
        out_specs=out_specs,
        check_vma=False,
    )
```

```python
import functools
import math

import jax
import jax.numpy as jnp
from jax import lax
from jax.experimental import pallas as pl
from jax.experimental.pallas import tpu as pltpu
from jax.sharding import PartitionSpec as P

MESH = pl.DeviceIdType.MESH
F32 = jnp.float32
BF16 = jnp.bfloat16
SUM = jnp.bfloat16

LEV = 16
C = 128
ROWS = 16
COLS = 128
HALO = 4
PITCH = COLS + 2 * HALO
FLAT = 26 * 128
LEAD = 128
OFFSETS = [(di, dj) for di in (-1, 0, 1) for dj in (-1, 0, 1)]
SHIFTS = [di * PITCH + dj for di, dj in OFFSETS]
PRED_FIRST = 2
PRED_TILES = 22
TAPS = 9 * LEV
VMEM_LIMIT = 40 * 1024 * 1024


def ring_order(count):
    return sorted(range(count), key=lambda d: (-min(d, count - d), d))


def shares(members):
    low, extra = divmod(PRED_TILES, members)
    return low, extra


def kernel(
    sizes,
    x_hbm,
    t_hbm,
    w_in_hbm,
    bias_ref,
    w_out_hbm,
    field,
    sums_ref,
    x16,
    t16,
    w_in_t,
    w_out,
    bias16,
    rows32,
    xf,
    w_in,
    w_out_t,
    bias,
    masks,
    side_send,
    band_send,
    side_recv,
    band_recv,
    xc,
    pre,
    act,
    act_t,
    xc_t,
    taps,
    pred_send,
    pred_recv,
    target_tiles,
    grads,
    grad_send,
    grad_recv,
    gp,
    gc,
    gh,
    gh_own,
    by_row,
    part_sum,
    part_recv,
    spare_recv,
    first,
    second,
    spare_first,
    spare_second,
    spare_all,
    all_recv,
    load_sem,
    send_sem,
    recv_sem,
    met_sem,
):
    members, lats, lons = sizes
    zs = members // 2
    quads = 2 * lats
    low, extra = shares(members)
    share = low + 1
    me_m = lax.axis_index("member")
    me_a = lax.axis_index("lat")
    me_o = lax.axis_index("lon")
    me_z = me_m // 2
    me_h = me_m % 2
    me_q = me_h * lats + me_a

    loads = [
        pltpu.make_async_copy(src, dst, load_sem.at[i])
        for i, (src, dst) in enumerate(
            (
                (x_hbm.at[0], x16),
                (t_hbm, t16),
                (w_in_hbm, w_in_t),
                (w_out_hbm, w_out),
                (bias_ref, bias16),
            )
        )
    ]
    for load in loads:
        load.start()

    def at(dm_z, dm_h, da, do):
        return (
            ((me_z + dm_z) % zs) * 2 + (me_h + dm_h) % 2,
            (me_a + da + lats) % lats,
            (me_o + do + lons) % lons,
        )

    halo = [(da, do) for da, do in ((-1, -1), (-1, 1), (1, -1), (1, 1), (0, -1), (0, 1), (-1, 0), (1, 0))]
    group_m = [(dz, h) for dz in ring_order(zs) for h in (1, 0) if dz or h]
    group_q = [(1, 0), (1, 1), (1, 3), (1, 2), (0, 2), (0, 1), (0, 3)]
    group_o = [d for d in ring_order(lons) if d]
    group_z = [d for d in ring_order(zs) if d]

    barrier = pltpu.get_barrier_semaphore()
    near = [at(0, 0, da, do) for da, do in halo] + [at(0, 1, 0, 0)]
    near += [at(dz, 0, 0, 0) for dz in (1, zs - 1, 2, zs - 2)] + [at(0, 0, 0, do) for do in (2, -2)]
    for device in near:
        pl.semaphore_signal(barrier, inc=1, device_id=device, device_id_type=MESH)

    steps = [at(dz, 0, 0, 0) for dz in (2, zs - 2, 1, zs - 1)] + [at(0, 0, 0, do) for do in (2, -2)]
    steps += [at(0, 0, da, 0) for da in (1, -1)]

    def tell(wave):
        for device in steps:
            pl.semaphore_signal(met_sem.at[wave], inc=1, device_id=device, device_id_type=MESH)

    def hear(wave):
        pl.semaphore_wait(met_sem.at[wave], len(steps))

    loads[0].wait()
    loads[1].wait()
    rows32[0:LEV] = x16[...].astype(F32)
    rows32[LEV:] = t16[...].astype(F32)
    for r in range(ROWS):
        start = LEAD + PITCH * (r + HALO) + HALO
        xf[:, start : start + COLS] = rows32[:, r, :]

    def place(first, height, width):
        lane = lax.broadcasted_iota(jnp.int32, (height, width), 1).astype(F32) + float(first)
        row = jnp.floor((lane + 0.5) * (1.0 / PITCH))
        return row, lane - PITCH * row

    for part in range(2):
        chans = slice(part * LEV, (part + 1) * LEV)
        left_edge = jnp.zeros((LEV, 128), F32)
        right_edge = jnp.zeros((LEV, 128), F32)
        for t in range(4, 22):
            row, col = place(t * 128, LEV, 128)
            here = (row >= HALO) & (row < HALO + ROWS)
            tile = xf[chans, LEAD + t * 128 : LEAD + t * 128 + 128]
            left_edge += jnp.where(here & (col >= HALO) & (col < 2 * HALO), tile, 0.0)
            right_edge += jnp.where(here & (col >= COLS) & (col < COLS + HALO), tile, 0.0)
        side_send[part, 0] = right_edge.astype(BF16)
        side_send[part, 1] = left_edge.astype(BF16)
        band_send[part, 0] = xf[chans, LEAD + 17 * 128 : LEAD + 22 * 128].astype(BF16)
        band_send[part, 1] = xf[chans, LEAD + 4 * 128 : LEAD + 9 * 128].astype(BF16)

    pl.semaphore_wait(barrier, len(near))

    def send(src, dst, phase, device):
        copy = pltpu.make_async_remote_copy(
            src_ref=src,
            dst_ref=dst,
            send_sem=send_sem.at[phase],
            recv_sem=recv_sem.at[phase],
            device_id=device,
            device_id_type=MESH,
        )
        copy.start()

    def wait_recv(ref, phase):
        pltpu.make_async_remote_copy(
            src_ref=ref,
            dst_ref=ref,
            send_sem=send_sem.at[phase],
            recv_sem=recv_sem.at[phase],
            device_id=(me_m, me_a, (me_o + 1) % lons),
            device_id_type=MESH,
        ).wait_recv()

    def wait_send(ref, phase):
        pltpu.make_async_remote_copy(
            src_ref=ref,
            dst_ref=ref,
            send_sem=send_sem.at[phase],
            recv_sem=recv_sem.at[phase],
            device_id=(me_m, me_a, (me_o + 1) % lons),
            device_id_type=MESH,
        ).wait_send()

    for part in range(2):
        for da in (-1, 1, 0):
            send(side_send.at[part, 0], side_recv.at[part, 0, 1 - da], 2 * part, at(0, 0, da, 1))
            send(side_send.at[part, 1], side_recv.at[part, 1, 1 - da], 2 * part, at(0, 0, da, -1))
        send(band_send.at[part, 0], band_recv.at[part, 0], 2 * part + 1, at(0, 0, 1, 0))
        send(band_send.at[part, 1], band_recv.at[part, 1], 2 * part + 1, at(0, 0, -1, 0))
    tell(0)

    for load in loads[2:]:
        load.wait()
    w_in[...] = w_in_t[...].astype(F32).T.astype(BF16)
    w_out_t[...] = w_out[...].astype(F32).T.astype(BF16)
    bias[...] = jnp.broadcast_to(bias16[...], (C, C)).T
    taps[:, 0:128] = jnp.zeros((TAPS, 128), F32)
    taps[:, FLAT - 128 : FLAT] = jnp.zeros((TAPS, 128), F32)
    xf[:, 0:LEAD] = jnp.zeros((2 * LEV, LEAD), F32)
    xf[:, LEAD + FLAT :] = jnp.zeros((2 * LEV, 128), F32)
    gp[:, 0 : PRED_FIRST * 128] = jnp.zeros((LEV, PRED_FIRST * 128), F32)
    gp[:, (PRED_FIRST + PRED_TILES) * 128 :] = jnp.zeros((LEV, PRED_FIRST * 128), F32)
    row_low = jnp.where(me_a == 0, HALO, 0).astype(F32)
    row_high = jnp.where(me_a == lats - 1, HALO + ROWS, ROWS + 2 * HALO).astype(F32)
    row, col = place(0, 8, FLAT)
    masks[0] = jnp.where((row >= row_low) & (row < row_high), 1.0, 0.0)
    masks[1] = jnp.where(
        (row >= HALO) & (row < HALO + ROWS) & (col >= HALO) & (col < HALO + COLS), 1.0, 0.0
    )

    hear(0)
    tell(1)
    wait_recv(side_recv.at[0], 0)
    wait_recv(band_recv.at[0], 1)

    def unpack(part):
        chans = slice(part * LEV, (part + 1) * LEV)
        sides = [[side_recv[part, i, j].astype(F32) for j in range(3)] for i in range(2)]
        for t in range(26):
            row, col = place(t * 128, LEV, 128)
            lanes = slice(LEAD + t * 128, LEAD + t * 128 + 128)
            tile = xf[chans, lanes]
            left, right = sides[0][1], sides[1][1]
            if t < 5:
                above = row < HALO
                band = band_recv[part, 0, :, t * 128 : t * 128 + 128].astype(F32)
                tile = jnp.where(above, band, tile)
                left = jnp.where(above, sides[0][0], left)
                right = jnp.where(above, sides[1][0], right)
            if t >= 21:
                below = row >= HALO + ROWS
                band = band_recv[part, 1, :, (t - 21) * 128 : (t - 20) * 128].astype(F32)
                tile = jnp.where(below, band, tile)
                left = jnp.where(below, sides[0][2], left)
                right = jnp.where(below, sides[1][2], right)
            tile = jnp.where(col < HALO, left, tile)
            tile = jnp.where(col >= HALO + COLS, right, tile)
            if t < 5 or t >= 21:
                tile = jnp.where((row >= row_low) & (row < row_high), tile, 0.0)
            if part == 0:
                xf[chans, lanes] = tile
            elif PRED_FIRST <= t < PRED_FIRST + PRED_TILES:
                target_tiles[t - PRED_FIRST] = tile

    unpack(0)
    for k, shift in enumerate(SHIFTS):
        xc[k * LEV : (k + 1) * LEV, 128:3200] = xf[0:LEV, LEAD + 128 + shift : LEAD + 3200 + shift].astype(BF16)

    def mask(which, first, last):
        return masks[which, 0:1, first:last] > 0.5

    hidden = jnp.dot(w_in[...], xc[:, 128:3200], preferred_element_type=F32)
    hidden += jnp.concatenate([bias[...]] * 24, axis=1)
    pre[:, 128:3200] = hidden
    value = jnp.where(mask(0, 128, 3200), hidden * jax.nn.sigmoid(hidden), 0.0).astype(BF16)
    act[:, 128:3200] = value
    taps[:, 128:3200] = jnp.dot(w_out[...], value, preferred_element_type=F32)

    def predict(t, count):
        begin, width = (PRED_FIRST + t) * 128, count * 128
        total = xf[0:LEV, LEAD + begin : LEAD + begin + width]
        for k, shift in enumerate(SHIFTS):
            total += taps[k * LEV : (k + 1) * LEV, begin + shift : begin + shift + width]
        for u in range(count):
            pred_send[t + u] = total[:, u * 128 : (u + 1) * 128].astype(BF16)

    def rank(z, h):
        return ((z + 3) % zs) * 2 + h

    def tiles_of(ref, slot, more):
        start = slot * share if more else extra + slot * low
        return ref.at[pl.ds(start, share if more else low)]

    def either(slot, act_on):
        @pl.when(slot < extra)
        def _():
            act_on(True, share)

        @pl.when(slot >= extra)
        def _():
            act_on(False, low)

    me_r = rank(me_z, me_h)
    def send_pred(more):
        for dz, h in group_m:
            device = at(dz, h, 0, 0)
            slot = rank(device[0] // 2, device[0] % 2)

            @pl.when(slot < extra if more else slot >= extra)
            def _(device=device, slot=slot):
                dst = pred_recv.at[me_m, pl.ds(0, share if more else low)]
                send(tiles_of(pred_send, slot, more), dst, 4, device)

    predict(0, extra * share)
    hear(1)
    send_pred(True)
    predict(extra * share, PRED_TILES - extra * share)
    send_pred(False)

    hidden = pre[:, 384:2944]
    gate = jax.nn.sigmoid(hidden)
    pre[:, 384:2944] = gate * (1.0 + hidden * (1.0 - gate))
    act_t[...] = jnp.where(mask(1, 512, 2816), act[:, 512:2816].astype(F32), 0.0).T.astype(BF16)
    xc_t[...] = xc[:, 512:2816].astype(F32).T.astype(BF16)
    wait_recv(side_recv.at[1], 2)
    wait_recv(band_recv.at[1], 3)
    unpack(1)

    coupling = (1.0 - 0.05 / members) / (members - 1)

    def slope(d):
        return d * lax.rsqrt(d * d + 0.25)

    def own_tiles(more, count):
        start = me_r * share if more else extra + me_r * low
        for u in range(count):
            pred_recv[me_m, u] = pred_send[start + u]
        wait_recv(pred_recv.at[pl.ds(0, members - 1), pl.ds(0, count)], 4)
        for u in range(count):
            everyone = pred_recv[:, u].astype(F32)
            wanted = target_tiles[start + u]
            for half in range(2):
                own = everyone[:, half * 8 : half * 8 + 8]
                spread = jnp.zeros_like(own)
                for d in range(1, members // 2 + 1):
                    term = slope(own - jnp.concatenate([own[d:], own[:d]], axis=0))
                    spread += term
                    if 2 * d != members:
                        spread -= jnp.concatenate([term[members - d :], term[: members - d]], axis=0)
                value = slope(own - wanted[None, half * 8 : half * 8 + 8]) - coupling * spread
                grads[:, half * 8 : half * 8 + 8, :] = value
            grad_send[:, u] = grads[...].astype(BF16)
            for dz, h in group_m:
                device = at(dz, h, 0, 0)
                send(grad_send.at[device[0], u], grad_recv.at[start + u], 5, device)
        for u in range(count):
            grad_recv[start + u] = grad_send[me_m, u]
        wait_recv(grad_recv.at[pl.ds(0, PRED_TILES - count)], 5)

    either(me_r, own_tiles)

    for u in range(PRED_TILES):
        t = PRED_FIRST + u
        row, col = place(t * 128, LEV, 128)
        inside = (row >= row_low) & (row < row_high) & (col >= HALO - 2) & (col < HALO + COLS + 2)
        tile = grad_recv[u].astype(F32)
        gp[:, t * 128 : t * 128 + 128] = jnp.where(inside, tile, 0.0)
    for k, shift in enumerate(SHIFTS):
        gc[k * LEV : (k + 1) * LEV, 384:2944] = gp[:, 384 - shift : 2944 - shift].astype(BF16)

    spare_owner = (0, quads - 1)

    def in_group(q):
        return (me_z * 2 + q // lats, q % lats, me_o)

    def spread_part(p, value):
        part_sum[p] = value.reshape(9, LEV, C).astype(SUM)
        for h, da in group_q:
            device = at(0, h, da, 0)
            slot = (device[0] % 2) * lats + device[1]
            send(part_sum.at[p, slot], part_recv.at[p, me_q], 6 + p, device)

        @pl.when(me_q != spare_owner[p])
        def _():
            send(part_sum.at[p, 8], spare_recv.at[me_q], 8 + p, in_group(spare_owner[p]))

        part_recv[p, me_q] = part_sum[p, me_q]

    def total_of(ref, count):
        total = ref[0].astype(F32)
        for i in range(1, count):
            total += ref[i].astype(F32)
        return total

    out_part = jnp.dot(gc[:, 512:2816], act_t[...], preferred_element_type=F32)
    spread_part(0, out_part)

    value = jnp.dot(w_out_t[...], gc[:, 384:2944], preferred_element_type=F32) * pre[:, 384:2944]
    gh_own[:, 384:2944] = jnp.where(mask(1, 384, 2944), value, 0.0).astype(BF16)
    gh[:, 384:2944] = jnp.where(mask(0, 384, 2944), value, 0.0).astype(BF16)
    in_part = jnp.dot(gh_own[:, 512:2816], xc_t[...], preferred_element_type=F32).T
    spread_part(1, in_part)

    taps[:, 384:2944] = jnp.dot(w_in_t[...], gh[:, 384:2944], preferred_element_type=F32)
    for r in range(ROWS):
        start = PITCH * (r + HALO) + HALO
        total = gp[:, start : start + COLS]
        for k, shift in enumerate(SHIFTS):
            total += taps[k * LEV : (k + 1) * LEV, start - shift : start - shift + COLS]
        by_row[r] = total

    by_lon = (me_o, lons, [at(0, 0, 0, d) for d in group_o])
    by_z = (me_z, zs, [at(d, 0, 0, 0) for d in group_z])
    first_axis, second_axis = (by_lon, by_z), (by_z, by_lon)

    def share_sum(value, dst, phase, axis):
        dst[axis[0]] = value.astype(SUM)
        for device in axis[2]:
            send(dst.at[axis[0]], dst.at[axis[0]], phase, device)

    for p in range(2):
        wait_recv(part_recv.at[p, pl.ds(0, quads - 1)], 6 + p)
        share_sum(total_of(part_recv.at[p], quads), first.at[p], 10 + p, first_axis[p])

        @pl.when(me_q == spare_owner[p])
        def _():
            spare_recv[me_q] = part_sum[p, 8]
            wait_recv(spare_recv.at[pl.ds(0, quads - 1)], 8 + p)
            share_sum(total_of(spare_recv, quads), spare_first, 14, first_axis[p])

    for level in range(LEV):
        field[level] = by_row[:, level, :]

    for p in range(2):
        count = first_axis[p][1]
        wait_recv(first.at[p, pl.ds(0, count - 1)], 10 + p)
        share_sum(total_of(first.at[p], count), second.at[p], 12 + p, second_axis[p])

        @pl.when(me_q == spare_owner[p])
        def _():
            wait_recv(spare_first.at[pl.ds(0, count - 1)], 14)
            share_sum(total_of(spare_first, count), spare_second, 15, second_axis[p])

    scale = 1.0 / math.sqrt(members * lats * lons * ROWS * COLS)
    for p in range(2):
        count = second_axis[p][1]
        wait_recv(second.at[p, pl.ds(0, count - 1)], 12 + p)
        all_recv[p, me_q] = (total_of(second.at[p], count) * scale).astype(SUM)
        for h, da in group_q:
            send(all_recv.at[p, me_q], all_recv.at[p, me_q], (16, 19)[p], at(0, h, da, 0))

        @pl.when(me_q == spare_owner[p])
        def _():
            wait_recv(spare_second.at[pl.ds(0, count - 1)], 15)
            spare_all[p] = (total_of(spare_second, count) * scale).astype(SUM)
            for h, da in group_q:
                send(spare_all.at[p], spare_all.at[p], 17 + p, at(0, h, da, 0))

    for part in range(2):
        wait_send(side_recv.at[part], 2 * part)
        wait_send(band_recv.at[part], 2 * part + 1)
    def all_sent(more, count):
        wait_send(pred_send.at[pl.ds(0, PRED_TILES - count)], 4)
        wait_send(grad_send.at[pl.ds(0, members - 1), pl.ds(0, count)], 5)

    either(me_r, all_sent)
    for p in range(2):
        wait_send(part_recv.at[p, pl.ds(0, quads - 1)], 6 + p)

        @pl.when(me_q != spare_owner[p])
        def _():
            wait_send(spare_recv.at[0], 8 + p)

    for p in range(2):
        wait_send(first.at[p, pl.ds(0, first_axis[p][1] - 1)], 10 + p)
        wait_send(second.at[p, pl.ds(0, second_axis[p][1] - 1)], 12 + p)

        @pl.when(me_q == spare_owner[p])
        def _():
            wait_send(spare_first.at[pl.ds(0, first_axis[p][1] - 1)], 14)
            wait_send(spare_second.at[pl.ds(0, second_axis[p][1] - 1)], 15)

    for p in range(2):
        wait_recv(all_recv.at[p, pl.ds(0, quads - 1)], (16, 19)[p])

        @pl.when(me_q != spare_owner[p])
        def _():
            wait_recv(spare_all.at[p], 17 + p)

        for t in range(8):
            sums_ref[p, t] = all_recv[p, t].astype(F32)
        sums_ref[p, 8] = spare_all[p].astype(F32)

    for p in range(2):
        wait_send(all_recv.at[p, pl.ds(0, quads - 1)], (16, 19)[p])

        @pl.when(me_q == spare_owner[p])
        def _():
            wait_send(spare_recv.at[pl.ds(0, quads - 1)], 17 + p)


def write_out(field, sums, field_out, gin_out, gout_out, sem):
    copies = [
        pltpu.make_async_copy(src, dst, sem.at[i])
        for i, (src, dst) in enumerate(
            ((field, field_out.at[0]), (sums.at[1], gin_out), (sums.at[0], gout_out))
        )
    ]
    for copy in copies:
        copy.start()
    for copy in copies:
        copy.wait()


def shards(sizes, inputs, target, conv_in, bias_in, conv_out):
    members, lats, lons = sizes
    quads = 2 * lats
    low, extra = shares(members)
    share = low + 1
    wide = FLAT + LEAD + 128
    anywhere = pl.BlockSpec(memory_space=pl.ANY)
    near = pl.BlockSpec(memory_space=pltpu.VMEM)
    field, sums = pl.pallas_call(
        functools.partial(kernel, sizes),
        out_shape=(
            pltpu.VMEM((LEV, ROWS, COLS), F32),
            pltpu.VMEM((2, 9, LEV, C), F32),
        ),
        in_specs=[pl.BlockSpec(memory_space=pltpu.HBM)] * 5,
        out_specs=(near, near),
        scratch_shapes=[
            pltpu.VMEM((LEV, ROWS, COLS), BF16),
            pltpu.VMEM((LEV, ROWS, COLS), BF16),
            pltpu.VMEM((TAPS, C), BF16),
            pltpu.VMEM((TAPS, C), BF16),
            pltpu.VMEM((1, C), F32),
            pltpu.VMEM((2 * LEV, ROWS, COLS), F32),
            pltpu.VMEM((2 * LEV, wide), F32),
            pltpu.VMEM((C, TAPS), BF16),
            pltpu.VMEM((C, TAPS), BF16),
            pltpu.VMEM((C, C), F32),
            pltpu.VMEM((2, 8, FLAT), F32),
            pltpu.VMEM((2, 2, LEV, 128), BF16),
            pltpu.VMEM((2, 2, LEV, 640), BF16),
            pltpu.VMEM((2, 2, 3, LEV, 128), BF16),
            pltpu.VMEM((2, 2, LEV, 640), BF16),
            pltpu.VMEM((TAPS, FLAT), BF16),
            pltpu.VMEM((C, FLAT), F32),
            pltpu.VMEM((C, FLAT), BF16),
            pltpu.VMEM((2304, C), BF16),
            pltpu.VMEM((2304, TAPS), BF16),
            pltpu.VMEM((TAPS, FLAT), F32),
            pltpu.VMEM((PRED_TILES, LEV, 128), BF16),
            pltpu.VMEM((members, share, LEV, 128), BF16),
            pltpu.VMEM((PRED_TILES, LEV, 128), F32),
            pltpu.VMEM((members, LEV, 128), F32),
            pltpu.VMEM((members, share, LEV, 128), BF16),
            pltpu.VMEM((PRED_TILES, LEV, 128), BF16),
            pltpu.VMEM((LEV, FLAT), F32),
            pltpu.VMEM((TAPS, FLAT), BF16),
            pltpu.VMEM((C, FLAT), BF16),
            pltpu.VMEM((C, FLAT), BF16),
            pltpu.VMEM((ROWS, LEV, COLS), F32),
            pltpu.VMEM((2, 9, LEV, C), SUM),
            pltpu.VMEM((2, quads, LEV, C), SUM),
            pltpu.VMEM((quads, LEV, C), SUM),
            pltpu.VMEM((2, max(lons, members // 2), LEV, C), SUM),
            pltpu.VMEM((2, max(lons, members // 2), LEV, C), SUM),
            pltpu.VMEM((max(lons, members // 2), LEV, C), SUM),
            pltpu.VMEM((max(lons, members // 2), LEV, C), SUM),
            pltpu.VMEM((2, LEV, C), SUM),
            pltpu.VMEM((2, quads, LEV, C), SUM),
            pltpu.SemaphoreType.DMA((5,)),
            pltpu.SemaphoreType.DMA((20,)),
            pltpu.SemaphoreType.DMA((20,)),
            pltpu.SemaphoreType.REGULAR((2,)),
        ],
        compiler_params=pltpu.CompilerParams(
            collective_id=0, has_side_effects=True, vmem_limit_bytes=VMEM_LIMIT
        ),
        name="downscaling_step",
    )(
        *(
            pltpu.with_memory_space_constraint(operand, pltpu.HBM)
            for operand in (
                inputs,
                target,
                conv_in.transpose(0, 2, 1).reshape(TAPS, C),
                bias_in.reshape(1, C),
                conv_out.reshape(TAPS, C),
            )
        )
    )
    field, gin, gout = pl.pallas_call(
        write_out,
        out_shape=(
            jax.ShapeDtypeStruct((1, LEV, ROWS, COLS), F32),
            jax.ShapeDtypeStruct((9, LEV, C), F32),
            jax.ShapeDtypeStruct((9, LEV, C), F32),
        ),
        in_specs=[near] * 2,
        out_specs=(anywhere,) * 3,
        scratch_shapes=[pltpu.SemaphoreType.DMA((3,))],
        compiler_params=pltpu.CompilerParams(vmem_limit_bytes=1024 * 1024),
        name="write_out",
    )(field, sums)
    return field, gin.transpose(0, 2, 1), gout


def solution(mesh):
    sizes = tuple(mesh.shape[axis] for axis in ("member", "lat", "lon"))
    in_specs = (P("member", None, "lat", "lon"), P(None, "lat", "lon"), P(), P(), P())
    out_specs = (P("member", None, "lat", "lon"), P(), P())
    return jax.shard_map(
        functools.partial(shards, sizes),
        mesh=mesh,
        in_specs=in_specs,
        out_specs=out_specs,
        check_vma=False,
    )
```
